32 devices in a mesh: seq: 16 (over z, x, core), head: 2 (over y).
Axes of the slice: x: 2, y: 2, z: 4, core: 2. Of those that a mesh axis runs over, the one named last changes fastest.
Arguments:
- tokens: bfloat16 [8192, 1024], P(('seq', 'head')), may hold values from -6 to 6
- w_query: bfloat16 [1024, 1024], P(None, 'head'), may hold values from -0.1875 to 0.1875
- w_key: bfloat16 [1024, 1024], P(None, 'head'), may hold values from -0.1875 to 0.1875
- w_value: bfloat16 [1024, 1024], P(None, 'head'), may hold values from -0.1875 to 0.1875
- w_beta: bfloat16 [1024, 8], P(None, 'head'), may hold values from -0.09375 to 0.09375
- beta_bias: float32 [8], P('head'), may hold values from -1 to 3, as said below
- conv_weight: float32 [3, 4, 1024], P(None, None, 'head'), may hold values from -3 to 3
- norm_gain: float32 [1024], P('head'), may hold values from 0.1 to 1.9
- w_out: bfloat16 [1024, 1024], P('head'), may hold values from -0.1875 to 0.1875
Outputs:
- mixed: bfloat16 [8192, 1024], P(('seq', 'head'))
The draws below stay inside these ranges and needn't reach their ends.
Inputs may be any that keep to these rules, and one draw needn't show every extreme that they name: `beta_bias`: one logit offset per head.
All inputs are finite; a program needn't handle non-finite values.
Results may differ from the reference program's by a relative error of at most 0.015.
The reference program's roundings to bfloat16 on the way (of `projected` and `normed`) count: a program that leaves them out, or rounds other values in their place, can miss the bound.
Values may be sent and summed in bfloat16 or wider, within the bound.
No kernel may reach another device: no remote copies, remote signals or barrier semaphores. Data moves between devices by JAX's collectives and lax.ppermute only.
A program may use at most 64 MiB of HBM per device.

```python
import jax
import jax.numpy as jnp
from jax import lax

D = 1024
HEADS = 8
HD = 128
CONV = 4
HEADS_DEV = 4
TOKENS = 8192
N_HEAD = 2


def draw_beta_bias(key, part):
    ranking = jax.random.permutation(jax.random.fold_in(key, 11), HEADS)
    spread = jax.random.uniform(jax.random.fold_in(key, 12), (HEADS,), jnp.float32)
    keeping = ranking < HEADS // 2
    return jnp.where(keeping, 2.0 + spread, -1.0 + 2.0 * spread)


def block_scale(rng, shape, pieces, smallest, top_value):
    loudness, own = 1.0, jax.random.fold_in(rng, 6)
    for position, parts in pieces:
        draws = jnp.exp(jax.random.uniform(jax.random.fold_in(own, position), (parts,), jnp.float32, smallest / len(pieces), top_value / len(pieces)))
        loudness = loudness * jnp.repeat(draws, shape[position] // parts).reshape([-1 if axis == position else 1 for axis in range(len(shape))])
    return loudness


def scatter_about(stream_key, shape, scale, reach, pieces=(), held_as=jnp.bfloat16):
    entries = jax.random.normal(stream_key, shape, jnp.float32) * scale
    if len(pieces) > 0:
        entries = block_scale(stream_key, shape, pieces, -0.22, 0.18) * entries
    return jnp.clip(entries, min=-reach, max=reach).astype(held_as)


def setup_inputs(seed: int = 0) -> dict:
    arg_keys = jax.random.split(jax.random.key(seed), 10)
    return {
        "tokens": scatter_about(arg_keys[0], (TOKENS, D), 1.0, 6.0, ((0, 32),)),
        "w_query": scatter_about(arg_keys[1], (D, HEADS * HD), D ** -0.5, 0.1875, ((1, 2),)),
        "w_key": scatter_about(arg_keys[2], (D, HEADS * HD), D ** -0.5, 0.1875, ((1, 2),)),
        "w_value": scatter_about(arg_keys[3], (D, HEADS * HD), D ** -0.5, 0.1875, ((1, 2),)),
        "w_beta": scatter_about(arg_keys[4], (D, HEADS), (4 * D) ** -0.5, 0.09375, ((1, 2),)),
        "beta_bias": draw_beta_bias(jax.random.fold_in(arg_keys[9], 71), 0),
        "conv_weight": scatter_about(arg_keys[6], (3, CONV, HEADS * HD), CONV ** -0.5, 3.0, ((2, 2),), jnp.float32),
        "norm_gain": jnp.clip(1.0 + 0.18 * jax.random.normal(arg_keys[7], (HEADS * HD,), jnp.float32), 0.1, 1.9),
        "w_out": scatter_about(arg_keys[8], (HEADS * HD, D), (HEADS * HD) ** -0.5, 0.1875, ((0, 2),)),
    }


precise = lax.Precision.HIGHEST

def convolve(projected, weight):
    length = projected.shape[0]
    padded = jnp.concatenate([jnp.zeros((CONV - 1, projected.shape[1]), jnp.float32), projected.astype(jnp.float32)], 0)
    mixed_conv = padded[0:length] * weight[0]
    for offset in range(1, CONV):
        mixed_conv = mixed_conv + padded[offset:offset + length] * weight[offset]
    return jax.nn.silu(mixed_conv).astype(jnp.bfloat16)

def reference(tokens, w_query, w_key, w_value, w_beta, beta_bias, conv_weight, norm_gain, w_out):
    length = tokens.shape[0]
    projected = [jnp.dot(tokens, weight, preferred_element_type=jnp.float32).astype(jnp.bfloat16) for weight in (w_query, w_key, w_value)]
    queries = convolve(projected[0], conv_weight[0]).reshape(length, HEADS, HD)
    keys_raw = convolve(projected[1], conv_weight[1]).reshape(length, HEADS, HD)
    values_in = convolve(projected[2], conv_weight[2]).reshape(length, HEADS, HD)
    logits = jnp.dot(tokens, w_beta, preferred_element_type=jnp.float32) + beta_bias
    beta_rate = 2.0 * jax.nn.sigmoid(logits)
    gain_rows = norm_gain.reshape(HEADS, HD)

    def advance(carried, inputs):
        query_t, key_t, value_t, rate_t = inputs
        key_unit = key_t.astype(jnp.float32)
        key_unit = key_unit / jnp.sqrt(lax.optimization_barrier(jnp.sum(key_unit * key_unit, -1, keepdims=True)) + 1e-06)
        predicted = jnp.einsum('hvk,hk->hv', carried, key_unit, precision=precise)
        change = rate_t[:, None] * (value_t.astype(jnp.float32) - predicted)
        carried = carried + change[:, :, None] * key_unit[:, None, :]
        output = jnp.einsum('hvk,hk->hv', carried, query_t.astype(jnp.float32), precision=precise)
        scaled = output * lax.rsqrt(lax.optimization_barrier(jnp.mean(output * output, -1, keepdims=True)) + 1e-05) * gain_rows
        return (carried, scaled.astype(jnp.bfloat16))
    initial = jnp.zeros((HEADS, HD, HD), jnp.float32)
    normed = lax.scan(advance, initial, (queries, keys_raw, values_in, beta_rate))[1]
    grouped = normed.reshape(length, N_HEAD, HEADS_DEV * HD)
    weights = w_out.reshape(N_HEAD, HEADS_DEV * HD, D)
    summed = jnp.zeros((length, D), jnp.float32)
    for group_index in range(N_HEAD):
        partial_sum = jnp.dot(grouped[:, group_index], weights[group_index], preferred_element_type=jnp.float32)
        rounded = lax.optimization_barrier(partial_sum.astype(jnp.bfloat16))
        summed = summed + rounded.astype(jnp.float32)
    return summed.astype(jnp.bfloat16)
```

```python
import functools

import jax
import jax.numpy as jnp
from jax import lax
from jax.experimental import pallas as pl
from jax.experimental.pallas import tpu as pltpu
from jax.sharding import PartitionSpec as P

BASE = 32
HALO = 16
F32 = jnp.float32
BF16 = jnp.bfloat16
VMEM = pl.BlockSpec(memory_space=pltpu.VMEM)
NN = ((1,), (0,))
NT = ((1,), (1,))
TN = ((0,), (0,))


def dot(left, right, dims=NN):
    return lax.dot_general(left, right, (dims, ((), ())), preferred_element_type=F32)


def split(wide):
    top = wide.astype(BF16)
    return top, (wide - top.astype(F32)).astype(BF16)


def dot_wide(left, right, dims=NN):
    left_top, left_rest = split(left)
    right_top, right_rest = split(right)
    return (
        dot(left_top, right_top, dims)
        + dot(left_rest, right_top, dims)
        + dot(left_top, right_rest, dims)
    )


def dot_half(left, right, dims=NN):
    left_top, left_rest = split(left)
    return dot(left_top, right, dims) + dot(left_rest, right, dims)


def invert(lower):
    size = lower.shape[0]
    lanes = 128
    row = lax.broadcasted_iota(jnp.int32, (BASE, lanes), 0)
    lane = lax.broadcasted_iota(jnp.int32, (BASE, lanes), 1)
    group = lane // BASE
    parts = []
    for start in range(0, size, lanes):
        window = lower[start : start + lanes, start : start + lanes]
        packed = jnp.zeros((BASE, lanes), F32)
        for index in range(lanes // BASE):
            packed = jnp.where(group == index, window[index * BASE : (index + 1) * BASE], packed)
        solved = (row == lane - group * BASE).astype(F32)
        for step in range(BASE - 1):
            column = jnp.take_along_axis(packed, group * BASE + step, axis=1)
            solved = solved - column * solved[step : step + 1, :]
        inverse = jnp.concatenate(
            [jnp.where(group == index, solved, 0.0) for index in range(lanes // BASE)], 0
        )
        row_full = lax.broadcasted_iota(jnp.int32, (lanes, lanes), 0)
        lane_full = lax.broadcasted_iota(jnp.int32, (lanes, lanes), 1)
        width = BASE
        while width < lanes:
            coupling = jnp.where(
                (row_full // (2 * width) == lane_full // (2 * width))
                & (row_full // width != lane_full // width),
                window,
                0.0,
            )
            inverse = inverse - dot_wide(inverse, dot_wide(coupling, inverse))
            width *= 2
        parts.append(inverse)
    width = lanes
    while width < size:
        joined = []
        for index in range(0, len(parts), 2):
            first, second = parts[index], parts[index + 1]
            start = index * width
            below = lower[start + width : start + 2 * width, start : start + width]
            corner = -dot_wide(second, dot_wide(below, first))
            joined.append(
                jnp.concatenate(
                    [
                        jnp.concatenate([first, jnp.zeros_like(first)], 1),
                        jnp.concatenate([corner, second], 1),
                    ],
                    0,
                )
            )
        parts = joined
        width *= 2
    return parts[0]


def part_kernel(
    x_ref,
    halo_ref,
    wq_ref,
    wk_ref,
    wv_ref,
    wb_ref,
    bias_ref,
    conv_ref,
    pair_ref,
    local_ref,
    reach_ref,
    proj_ref,
):
    rows = x_ref.shape[0]
    heads = pair_ref.shape[0]
    dim = pair_ref.shape[2]
    taps = conv_ref.shape[1]
    x = x_ref[...]
    active = []
    for index, w_ref in enumerate((wq_ref, wk_ref, wv_ref)):
        proj_ref[index, :HALO] = dot(halo_ref[...], w_ref[...]).astype(BF16).astype(F32)
        proj_ref[index, HALO:] = dot(x, w_ref[...]).astype(BF16).astype(F32)
        first = HALO - (taps - 1)
        total = proj_ref[index, first : first + rows] * conv_ref[index, 0:1]
        for tap in range(1, taps):
            total = total + proj_ref[index, first + tap : first + tap + rows] * conv_ref[
                index, tap : tap + 1
            ]
        active.append((total / (1.0 + jnp.exp(-total))).astype(BF16))
    logits = dot(x, wb_ref[...]) + bias_ref[...]
    rates = 2.0 / (1.0 + jnp.exp(-logits))
    row = lax.broadcasted_iota(jnp.int32, (rows, rows), 0)
    lane = lax.broadcasted_iota(jnp.int32, (rows, rows), 1)
    for head in range(heads):
        span = slice(head * dim, (head + 1) * dim)
        query, key, value = (each[:, span] for each in active)
        rate = rates[:, head : head + 1]
        wide_key = key.astype(F32)
        norm = lax.rsqrt(jnp.sum(wide_key * wide_key, 1, keepdims=True) + 1e-6)
        norm_row = jnp.sum(jnp.where(row == lane, norm, 0.0), 0, keepdims=True)
        rate_row = jnp.sum(jnp.where(row == lane, rate, 0.0), 0, keepdims=True)
        gram = dot(key, key, NT)
        lower = jnp.where(row > lane, gram * (rate * norm) * norm_row, 0.0)
        inverse = invert(lower) * rate_row
        fresh = dot_half(inverse, value)
        weight = dot_half(inverse * norm_row, key)
        moved = dot_half(jnp.concatenate([weight * norm, fresh * norm], 1), key, TN)
        eye = (row[:dim, :dim] == lane[:dim, :dim]).astype(F32)
        pair_ref[head, :dim] = eye - moved[:dim]
        pair_ref[head, dim:] = moved[dim:]
        attend = jnp.where(row >= lane, dot(query, key, NT) * norm_row, 0.0)
        seen = dot_wide(attend, jnp.concatenate([fresh, weight], 1))
        local_ref[:, span] = seen[:, :dim]
        reach_ref[:, span] = query.astype(F32) - seen[:, dim:]


def compose(low, high):
    dim = low.shape[1]
    joined = dot_wide(low, high[:dim])
    return jnp.concatenate([joined[:dim], joined[dim:] + high[dim:]], 0)


def shard_kernel(flags_ref, own_ref, other_ref, first_ref, keep_ref, send_ref):
    heads = own_ref.shape[0]
    swapped = flags_ref[0] == 1
    kept = keep_ref.shape[0]
    bit = flags_ref[1]
    for head in range(heads):
        own, other = own_ref[head], other_ref[head]
        low = jnp.where(swapped, other, own)
        high = jnp.where(swapped, own, other)
        first_ref[head] = low
        whole = compose(low, high)
        if kept == heads:
            keep_ref[head] = whole
            send_ref[head] = whole.astype(BF16)
        else:
            side = head // kept

            @pl.when(bit == side)
            def _():
                keep_ref[head % kept] = whole

            @pl.when(bit != side)
            def _():
                send_ref[head % kept] = whole.astype(BF16)


def join_kernel(flags_ref, own_ref, other_ref, low_ref, total_ref, send_ref):
    later = flags_ref[0] == 1
    for head in range(own_ref.shape[0]):
        own, other = own_ref[head], other_ref[head].astype(F32)
        low = jnp.where(later, other, own)
        high = jnp.where(later, own, other)
        whole = compose(low, high)
        low_ref[head] = low
        total_ref[head] = whole
        start = whole.shape[0] - send_ref.shape[1]
        send_ref[head] = whole[start:].astype(BF16)


def enter_kernel(flags_ref, state_ref, *refs):
    levels = len(refs) - 2
    keep_ref, send_ref = refs[levels:]
    count = keep_ref.shape[0]
    dim = keep_ref.shape[1]
    for head in range(count):
        state = jnp.where(flags_ref[levels] == 1, state_ref[head].astype(F32), 0.0)
        for level in range(levels - 1, 0, -1):
            low = refs[level][head]
            after = dot_wide(state, low[:dim]) + low[dim:]
            state = jnp.where(flags_ref[level] == 1, after, state)
        low = refs[0][head]
        after = dot_wide(state, low[:dim]) + low[dim:]
        later = flags_ref[0] == 1
        keep_ref[head] = jnp.where(later, after, state)
        send_ref[head] = jnp.where(later, state, after).astype(BF16)


def finish_kernel(
    flags_ref, keep_ref, came_ref, first_ref, local0, local1, reach0, reach1, gain_ref, own_ref, other_ref
):
    heads = first_ref.shape[0]
    dim = first_ref.shape[2]
    count = keep_ref.shape[0]
    swapped = flags_ref[0] == 1
    bit = flags_ref[1]
    for head in range(heads):
        span = slice(head * dim, (head + 1) * dim)
        state = keep_ref[head % count]
        if count < heads:
            state = jnp.where(bit == head // count, state, came_ref[head % count].astype(F32))
        first = first_ref[head]
        middle = dot_wide(state, first[:dim]) + first[dim:]
        for local, reach, out, late in (
            (local0, reach0, own_ref, swapped),
            (local1, reach1, other_ref, jnp.logical_not(swapped)),
        ):
            entering = jnp.where(late, middle, state)
            rows = local[:, span] + dot_wide(reach[:, span], entering, NT)
            scale = lax.rsqrt(jnp.mean(rows * rows, 1, keepdims=True) + 1e-5)
            out[:, span] = (rows * scale * gain_ref[:, span]).astype(BF16)


def output_kernel(mine_ref, theirs_ref, w_mine_ref, w_theirs_ref, out_ref):
    mine = dot(mine_ref[...], w_mine_ref[...]).astype(BF16).astype(F32)
    theirs = dot(theirs_ref[...], w_theirs_ref[...]).astype(BF16).astype(F32)
    out_ref[...] = (mine + theirs).astype(BF16)


def call(kernel, outs, inputs, flags=None, scratch=(), flops=0, moved=0):
    specs = [VMEM] * len(inputs)
    if flags is not None:
        inputs = [flags] + list(inputs)
        specs = [pl.BlockSpec(memory_space=pltpu.SMEM)] + specs
    return pl.pallas_call(
        kernel,
        out_shape=[jax.ShapeDtypeStruct(shape, dtype) for shape, dtype in outs],
        in_specs=specs,
        out_specs=[VMEM] * len(outs),
        scratch_shapes=list(scratch),
        compiler_params=pltpu.CompilerParams(vmem_limit_bytes=48 * 1024 * 1024),
        cost_estimate=pl.CostEstimate(flops=flops, bytes_accessed=moved, transcendentals=0),
    )(*inputs)


def shift(block, axes, pairs):
    return lax.ppermute(block, axes, pairs)


def local(tokens, w_query, w_key, w_value, w_beta, beta_bias, conv_weight, norm_gain, w_out):
    groups = lax.axis_size("head")
    shards = lax.axis_size("seq")
    heads = beta_bias.shape[0]
    columns = w_query.shape[1]
    dim = columns // heads
    width = tokens.shape[1]
    me_head = lax.axis_index("head")
    me_seq = lax.axis_index("seq")
    ahead = [(i, i + 1) for i in range(shards - 1)]

    if groups == 2:
        rows = tokens.shape[0]
        swap = [(0, 1), (1, 0)]
        tail = tokens[rows - HALO :]
        other = shift(tokens, "head", swap)
        flat = [(i, i + 1) for i in range(shards * groups - 1)]
        own_halo = shift(tail, ("seq", "head"), flat)
        behind = shift(tail, "seq", ahead)
        other_halo = jnp.where(me_head == 0, tail, behind)
        halves = [(tokens, own_halo), (other, other_halo)]
        swapped = me_head
    else:
        gathered = lax.all_gather(tokens, "head", axis=0, tiled=True)
        rows = gathered.shape[0] // 2
        behind = shift(gathered[2 * rows - HALO :], "seq", ahead)
        halves = [(gathered[:rows], behind), (gathered[rows:], gathered[rows - HALO : rows])]
        swapped = jnp.zeros((), jnp.int32)

    bias = beta_bias.reshape(1, heads)
    gain = norm_gain.reshape(1, columns)
    pair_shape = (heads, 2 * dim, dim)
    results = []
    for block, halo in halves:
        results.append(
            call(
                part_kernel,
                [(pair_shape, F32), ((rows, columns), F32), ((rows, columns), F32)],
                [block, halo, w_query, w_key, w_value, w_beta, bias, conv_weight],
                scratch=[pltpu.VMEM((3, rows + HALO, columns), F32)],
                flops=8 * 10**9,
                moved=5 * 10**6,
            )
        )
    (pair0, local0, reach0), (pair1, local1, reach1) = results

    levels = shards.bit_length() - 1
    bits = [(me_seq >> level) & 1 for level in range(levels)]
    kept = heads // 2 if heads % 2 == 0 else heads
    flags = jnp.stack([swapped, bits[0]]).astype(jnp.int32)
    first, keep, send = call(
        shard_kernel,
        [(pair_shape, F32), ((kept,) + pair_shape[1:], F32), ((kept,) + pair_shape[1:], BF16)],
        [pair0, pair1],
        flags=flags,
    )
    lows = []
    for level in range(levels):
        partner = [(i, i ^ (1 << level)) for i in range(shards)]
        if level == levels - 1:
            lows.append(shift(send, "seq", [(i, j) for i, j in partner if j > i]))
            break
        came = shift(send, "seq", partner)
        last = level == levels - 2
        low, keep, send = call(
            join_kernel,
            [
                (keep.shape, F32),
                (keep.shape, F32),
                ((kept, dim if last else 2 * dim, dim), BF16),
            ],
            [keep, came],
            flags=bits[level].reshape(1).astype(jnp.int32),
        )
        lows.append(low)
    state_in = lows.pop()
    keep, send = call(
        enter_kernel,
        [((kept, dim, dim), F32), ((kept, dim, dim), BF16)],
        [state_in] + lows,
        flags=jnp.stack(bits).astype(jnp.int32),
    )
    if kept < heads:
        came = shift(send, "seq", [(i, i ^ 1) for i in range(shards)])
    else:
        came = send
    normed0, normed1 = call(
        finish_kernel,
        [((rows, columns), BF16), ((rows, columns), BF16)],
        [keep, came, first, local0, local1, reach0, reach1, gain],
        flags=flags,
    )
    if groups == 2:
        w_other = shift(w_out, "head", swap)
        theirs = shift(normed1, "head", swap)
        return call(
            output_kernel,
            [((rows, width), BF16)],
            [normed0, theirs, w_out, w_other],
        )[0]
    normed = jnp.concatenate([normed0, normed1], 0)
    mine = jnp.dot(normed, w_out, preferred_element_type=F32).astype(BF16)
    return lax.psum_scatter(mine, "head", scatter_dimension=0, tiled=True)


def solution(mesh):
    in_specs = (
        P(("seq", "head"), None),
        P(None, "head"),
        P(None, "head"),
        P(None, "head"),
        P(None, "head"),
        P("head"),
        P(None, None, "head"),
        P("head"),
        P("head", None),
    )
    out_specs = P(("seq", "head"), None)
    return jax.shard_map(local, mesh=mesh, in_specs=in_specs, out_specs=out_specs, check_vma=False)
```

```python
import functools

import jax
import jax.numpy as jnp
from jax import lax
from jax.experimental import pallas as pl
from jax.experimental.pallas import tpu as pltpu
from jax.sharding import PartitionSpec as P

BASE = 16
HALO = 16
F32 = jnp.float32
BF16 = jnp.bfloat16
VMEM = pl.BlockSpec(memory_space=pltpu.VMEM)
NN = ((1,), (0,))
NT = ((1,), (1,))
TN = ((0,), (0,))


def dot(left, right, dims=NN):
    return lax.dot_general(left, right, (dims, ((), ())), preferred_element_type=F32)


def split(wide):
    top = wide.astype(BF16)
    return top, (wide - top.astype(F32)).astype(BF16)


def dot_wide(left, right, dims=NN):
    left_top, left_rest = split(left)
    right_top, right_rest = split(right)
    return (
        dot(left_top, right_top, dims)
        + dot(left_rest, right_top, dims)
        + dot(left_top, right_rest, dims)
    )


def dot_half(left, right, dims=NN):
    left_top, left_rest = split(left)
    return dot(left_top, right, dims) + dot(left_rest, right, dims)


def substitute(windows):
    lanes = windows[0].shape[0]
    row = lax.broadcasted_iota(jnp.int32, (8, lanes), 0)
    lane = lax.broadcasted_iota(jnp.int32, (8, lanes), 1)
    group = lane // BASE
    bands = BASE // 8
    packed, solved = [], []
    for window in windows:
        rows = []
        for band in range(bands):
            piece = window[band * 8 : band * 8 + 8]
            for index in range(1, lanes // BASE):
                start = index * BASE + band * 8
                piece = jnp.where(group == index, window[start : start + 8], piece)
            rows.append(piece)
        packed.append(rows)
        solved.append(
            [(row + band * 8 == lane - group * BASE).astype(F32) for band in range(bands)]
        )
    for step in range(BASE - 1):
        at = step // 8
        place = group * BASE + step
        for rows, found in zip(packed, solved):
            pivot = found[at][step % 8 : step % 8 + 1]
            for band in range(at, bands):
                if band > at or step % 8 < 7:
                    column = jnp.take_along_axis(rows[band], place, axis=1)
                    found[band] = found[band] - column * pivot
    return [
        jnp.concatenate(
            [jnp.where(group == index, piece, 0.0) for index in range(lanes // BASE) for piece in found],
            0,
        )
        for found in solved
    ]


def invert(lowers):
    size = lowers[0].shape[0]
    lanes = 128
    starts = range(0, size, lanes)
    windows = [low[at : at + lanes, at : at + lanes] for low in lowers for at in starts]
    inverses = substitute(windows)
    row = lax.broadcasted_iota(jnp.int32, (lanes, lanes), 0)
    lane = lax.broadcasted_iota(jnp.int32, (lanes, lanes), 1)
    width = BASE
    while width < lanes:
        mask = (row // (2 * width) == lane // (2 * width)) & (row // width != lane // width)
        inner = [
            dot_wide(jnp.where(mask, window, 0.0), inverse)
            for window, inverse in zip(windows, inverses)
        ]
        inverses = [inverse - dot_wide(inverse, each) for inverse, each in zip(inverses, inner)]
        width *= 2
    count = len(starts)
    groups = [inverses[at : at + count] for at in range(0, len(inverses), count)]
    while width < size:
        joined = []
        below = [
            [
                dot_wide(
                    low[(at + 1) * width : (at + 2) * width, at * width : (at + 1) * width], parts[at]
                )
                for at in range(0, len(parts), 2)
            ]
            for low, parts in zip(lowers, groups)
        ]
        for inner, parts in zip(below, groups):
            merged = []
            for at in range(0, len(parts), 2):
                first, second = parts[at], parts[at + 1]
                corner = -dot_wide(second, inner[at // 2])
                merged.append(
                    jnp.concatenate(
                        [
                            jnp.concatenate([first, jnp.zeros_like(first)], 1),
                            jnp.concatenate([corner, second], 1),
                        ],
                        0,
                    )
                )
            joined.append(merged)
        groups = joined
        width *= 2
    return [parts[0] for parts in groups]


def activate(x, weights, conv_ref, proj_ref, blocks):
    taps = conv_ref.shape[1]
    active = [[] for _ in blocks]
    for index, w_ref in enumerate(weights):
        proj_ref[index] = dot(x, w_ref[...]).astype(BF16).astype(F32)
        for (start, rows), outs in zip(blocks, active):
            first = start - (taps - 1)
            total = proj_ref[index, first : first + rows] * conv_ref[index, 0:1]
            for tap in range(1, taps):
                total = total + proj_ref[index, first + tap : first + tap + rows] * conv_ref[
                    index, tap : tap + 1
                ]
            outs.append((total / (1.0 + jnp.exp(-total))).astype(BF16))
    return active


def invert_few(count, lowers):
    inverses = []
    for lower in lowers:
        eye = jnp.eye(lower.shape[0], dtype=F32)
        inverse = eye - lower
        for _ in range(count - 2):
            inverse = eye - dot_wide(lower, inverse)
        inverses.append(inverse)
    return inverses


def transitions(keys, values, rates, invert=invert):
    rows, dim = keys[0].shape
    row = lax.broadcasted_iota(jnp.int32, (rows, rows), 0)
    lane = lax.broadcasted_iota(jnp.int32, (rows, rows), 1)
    norms, norm_rows, rate_rows, lowers = [], [], [], []
    for key, rate_row in zip(keys, rates):
        rate = jnp.sum(jnp.where(row == lane, rate_row, 0.0), 1, keepdims=True)
        wide_key = key.astype(F32)
        norm = lax.rsqrt(jnp.sum(wide_key * wide_key, 1, keepdims=True) + 1e-6)
        norm_row = jnp.sum(jnp.where(row == lane, norm, 0.0), 0, keepdims=True)
        norms.append(norm)
        norm_rows.append(norm_row)
        rate_rows.append(rate_row)
        gram = dot(key, key, NT)
        lowers.append(jnp.where(row > lane, gram * (rate * norm) * norm_row, 0.0))
    inverses = [each * rate for each, rate in zip(invert(lowers), rate_rows)]
    eye = jnp.eye(dim, dtype=F32)
    solved = []
    for key, value, inverse, norm_row in zip(keys, values, inverses, norm_rows):
        fresh = dot_half(inverse, value)
        weight = dot_half(inverse * norm_row, key)
        solved.append(jnp.concatenate([fresh, weight], 1))
    pairs = []
    for key, each, norm in zip(keys, solved, norms):
        moved = dot_half(each * norm, key, TN)
        pairs.append(jnp.concatenate([eye - moved[dim:], moved[:dim]], 0))
    return pairs, solved, norm_rows


def look(query, key, norm_row, solved):
    rows, dim = query.shape
    row = lax.broadcasted_iota(jnp.int32, (rows, rows), 0)
    lane = lax.broadcasted_iota(jnp.int32, (rows, rows), 1)
    attend = jnp.where(row >= lane, dot(query, key, NT) * norm_row, 0.0)
    seen = dot(attend.astype(BF16), solved)
    return jnp.concatenate([seen[:, :dim], query.astype(F32) - seen[:, dim:]], 1)


def spans_of(count, width):
    dim = width // count
    return [slice(head * dim, (head + 1) * dim) for head in range(count)]


def write_rates(x, wb, bias_ref):
    logits = dot(wb, x, NT)
    return [
        2.0 / (1.0 + jnp.exp(-(logits[head : head + 1] + bias_ref[head])))
        for head in range(wb.shape[0])
    ]


def edge_kernel(x_ref, head_ref, tail_ref):
    head_ref[...] = x_ref[: head_ref.shape[0]]
    tail_ref[...] = x_ref[x_ref.shape[0] - tail_ref.shape[0] :]


def early_kernel(
    bias_ref, x_ref, wq_ref, wk_ref, wv_ref, wb_ref, conv_ref, pair_ref, look_ref, proj_ref
):
    rows, width = x_ref.shape
    x = jnp.concatenate([jnp.zeros((HALO, width), BF16), x_ref[...]], 0)
    active = activate(x, (wq_ref, wk_ref, wv_ref), conv_ref, proj_ref, [(HALO, rows)])[0]
    spans = spans_of(pair_ref.shape[0], active[0].shape[1])
    queries, keys, values = ([each[:, span] for span in spans] for each in active)
    lane = lax.broadcasted_iota(jnp.int32, (1, rows), 1)
    rates = [
        jnp.where(lane < conv_ref.shape[1] - 1, 0.0, each)
        for each in write_rates(x_ref[...], wb_ref[...], bias_ref)
    ]
    pairs, solved, norm_rows = transitions(keys, values, rates)
    for head in range(len(spans)):
        pair_ref[head] = pairs[head]
        look_ref[head] = look(
            queries[head], keys[head], norm_rows[head], solved[head].astype(BF16)
        )


def late_kernel(
    flags_ref,
    bias_ref,
    x_ref,
    wq_ref,
    wk_ref,
    wv_ref,
    wb_ref,
    conv_ref,
    head_ref,
    tail_ref,
    halo_ref,
    behind_ref,
    early_ref,
    keep_ref,
    send_ref,
    norm_ref,
    held_ref,
    mini_ref,
    proj_ref,
):
    heads = early_ref.shape[0]
    kept = keep_ref.shape[0]
    rows = x_ref.shape[0]
    swapped = flags_ref[0] == 1
    halo = jnp.where(swapped, behind_ref[...], tail_ref[...])
    x = jnp.concatenate([halo, x_ref[...], halo_ref[...], head_ref[...]], 0)
    active, few = activate(
        x,
        (wq_ref, wk_ref, wv_ref),
        conv_ref,
        proj_ref,
        [(HALO, rows), (2 * HALO + rows, HALO)],
    )
    spans = spans_of(heads, active[0].shape[1])
    queries, keys, values = ([each[:, span] for span in spans] for each in active)
    rates = write_rates(x_ref[...], wb_ref[...], bias_ref)
    lane = lax.broadcasted_iota(jnp.int32, (1, HALO), 1)
    few_rates = [
        jnp.where(lane < conv_ref.shape[1] - 1, each, 0.0)
        for each in write_rates(head_ref[...], wb_ref[...], bias_ref)
    ]
    few_queries, few_keys, few_values = ([each[:, span] for span in spans] for each in few)
    few_pairs, few_solved, few_norm_rows = transitions(
        few_keys, few_values, few_rates, functools.partial(invert_few, conv_ref.shape[1] - 1)
    )
    early = []
    for head in range(heads):
        mini_ref[head] = look(
            few_queries[head], few_keys[head], few_norm_rows[head], few_solved[head].astype(BF16)
        )
        early.append(compose(few_pairs[head], early_ref[head]))
    pairs, solved, norm_rows = transitions(keys, values, rates)
    bit = flags_ref[1]
    wholes = []
    for head, late in enumerate(pairs):
        norm_ref[head : head + 1] = norm_rows[head]
        low = jnp.where(swapped, late, early[head])
        held_ref[head] = jnp.concatenate(
            [
                solved[head].astype(BF16),
                queries[head],
                keys[head],
                low.astype(BF16),
                few_pairs[head].astype(BF16),
            ],
            1,
        )
        wholes.append(compose(low, jnp.where(swapped, early[head], late)).astype(BF16))
    for head in range(kept):
        if kept == heads:
            keep_ref[head] = wholes[head]
            send_ref[head] = wholes[head]
        else:
            one, two = wholes[head], wholes[head + kept]
            keep_ref[head] = jnp.where(bit == 1, two, one)
            send_ref[head] = jnp.where(bit == 1, one, two)


def look_kernel(taps, flags_ref, norm_ref, held_ref, mini_ref, early_ref, both_ref):
    swapped = flags_ref[0] == 1
    heads = held_ref.shape[0]
    rows = held_ref.shape[1]
    dim = held_ref.shape[2] // 6
    row = lax.broadcasted_iota(jnp.int32, (HALO, 2 * dim), 0)
    for head in range(heads):
        late = look(
            held_ref[head, :, 2 * dim : 3 * dim],
            held_ref[head, :, 3 * dim : 4 * dim],
            norm_ref[head : head + 1],
            held_ref[head, :, : 2 * dim],
        )
        early = early_ref[head]
        few = held_ref[head, :, 5 * dim :]
        through = dot(early[:, dim:].astype(BF16), few, NT)
        early = jnp.concatenate([early[:, :dim] + through[:, dim:], through[:, :dim]], 1)
        top = jnp.where(row < taps - 1, mini_ref[head], early[:HALO])
        early = jnp.concatenate([top, early[HALO:]], 0)
        first = held_ref[head, :, 4 * dim : 5 * dim]
        later = jnp.where(swapped, early, late)
        through = dot(later[:, dim:].astype(BF16), first, NT)
        later = jnp.concatenate([later[:, :dim] + through[:, dim:], through[:, :dim]], 1)
        both_ref[0, head] = jnp.where(swapped, later, early)
        both_ref[1, head] = jnp.where(swapped, late, later)


def compose(low, high):
    dim = low.shape[1]
    joined = dot_wide(low, high[:dim])
    return jnp.concatenate([joined[:dim], joined[dim:] + high[dim:]], 0)


def join_kernel(flags_ref, own_ref, other_ref, send_ref):
    later = flags_ref[0] == 1
    for head in range(own_ref.shape[0]):
        own, other = own_ref[head], other_ref[head]
        low = jnp.where(later, other, own)
        high = jnp.where(later, own, other)
        dim = low.shape[1]
        joined = dot(low, high[:dim])
        start = 2 * dim - send_ref.shape[1]
        if start < dim:
            send_ref[head, : dim - start] = joined[start:dim].astype(BF16)
        send_ref[head, dim - start :] = (joined[dim:] + high[dim:].astype(F32)).astype(BF16)


def open_kernel(flags_ref, own_ref, other_ref, path_ref):
    dim = own_ref.shape[2]
    row = lax.broadcasted_iota(jnp.int32, (2 * dim, dim), 0)
    lane = lax.broadcasted_iota(jnp.int32, (2 * dim, dim), 1)
    for head in range(own_ref.shape[0]):
        path_ref[head, :, :dim] = (row == lane).astype(F32)
        low = jnp.where(flags_ref[0] == 1, other_ref[head], own_ref[head])
        path_ref[head, :, dim:] = low.astype(F32)


def path_kernel(flags_ref, path_ref, came_ref, out_ref):
    dim = came_ref.shape[2]
    for head in range(came_ref.shape[0]):
        path = path_ref[head]
        through = dot_wide(came_ref[head].astype(F32), path[:dim])
        longer = jnp.concatenate([through[:dim], through[dim:] + path[dim:]], 0)
        out_ref[head] = jnp.where(flags_ref[0] == 1, longer, path)


def enter_kernel(flags_ref, state_ref, path_ref, keep_ref, send_ref):
    dim = state_ref.shape[2]
    for head in range(keep_ref.shape[0]):
        state = jnp.where(flags_ref[1] == 1, state_ref[head], jnp.zeros_like(state_ref[head]))
        path = path_ref[head]
        both = (dot(state, path[:dim].astype(BF16)) + path[dim:]).astype(BF16)
        later = flags_ref[0] == 1
        keep_ref[head] = jnp.where(later, both[:, dim:], both[:, :dim])
        send_ref[head] = jnp.where(later, both[:, :dim], both[:, dim:])


def finish_kernel(place, flags_ref, keep_ref, came_ref, both_ref, gain_ref, out_ref):
    count, dim = keep_ref.shape[:2]
    heads = both_ref.shape[1]
    for head, span in enumerate(spans_of(heads, heads * dim)):
        state = keep_ref[head % count]
        if count < heads:
            state = jnp.where(flags_ref[0] == head // count, state, came_ref[head % count])
        reach = both_ref[place, head, :, dim:].astype(BF16)
        rows = both_ref[place, head, :, :dim] + dot(reach, state, NT)
        scale = lax.rsqrt(jnp.mean(rows * rows, 1, keepdims=True) + 1e-5)
        out_ref[:, span] = (rows * scale * gain_ref[:, span]).astype(BF16)


def finish_mine_kernel(flags_ref, keep_ref, came_ref, both_ref, gain_ref, w_ref, out_ref, normed_ref):
    finish_kernel(0, flags_ref, keep_ref, came_ref, both_ref, gain_ref, normed_ref)
    out_ref[...] = dot(normed_ref[...], w_ref[...]).astype(BF16)


def half_kernel(flags_ref, w_ref, part_ref):
    rows = part_ref.shape[0]
    part_ref[...] = w_ref[pl.ds(pl.multiple_of(flags_ref[0] * rows, rows), rows)]


def output_kernel(flags_ref, theirs_ref, part_ref, rest_ref, mine_ref, out_ref):
    rows = part_ref.shape[0]
    later = flags_ref[0] == 1
    low, high = theirs_ref[:, :rows], theirs_ref[:, rows:]
    total = dot(jnp.where(later, high, low), part_ref[...])
    total = total + dot(jnp.where(later, low, high), rest_ref[...])
    theirs = total.astype(BF16).astype(F32)
    out_ref[...] = (mine_ref[...].astype(F32) + theirs).astype(BF16)


def call(kernel, outs, inputs, scalars=(), scratch=(), flops=10**7, moved=10**5, grant=8):
    specs = [pl.BlockSpec(memory_space=pltpu.SMEM)] * len(scalars)
    specs += [VMEM] * len(inputs)
    return pl.pallas_call(
        kernel,
        out_shape=[jax.ShapeDtypeStruct(shape, dtype) for shape, dtype in outs],
        in_specs=specs,
        out_specs=[VMEM] * len(outs),
        scratch_shapes=list(scratch),
        compiler_params=pltpu.CompilerParams(vmem_limit_bytes=grant * 1024 * 1024),
        cost_estimate=pl.CostEstimate(flops=flops, bytes_accessed=moved, transcendentals=0),
    )(*scalars, *inputs)


def together(*arrays):
    return lax.optimization_barrier(arrays)


def shift(block, axes, pairs):
    return lax.ppermute(block, axes, pairs)


def local(tokens, w_query, w_key, w_value, w_beta, beta_bias, conv_weight, norm_gain, w_out):
    groups = lax.axis_size("head")
    shards = lax.axis_size("seq")
    heads = beta_bias.shape[0]
    columns = w_query.shape[1]
    dim = columns // heads
    width = tokens.shape[1]
    me_head = lax.axis_index("head")
    me_seq = lax.axis_index("seq")
    ahead = [(i, i + 1) for i in range(shards - 1)]

    if groups == 2:
        rows = tokens.shape[0]
        swap = [(0, 1), (1, 0)]
        early = tokens
        late = shift(tokens, "head", swap)
        head, tail = call(
            edge_kernel, [((HALO, width), BF16)] * 2, [tokens], flops=2 * 10**10, moved=10**6
        )
        flat = [(i, i + 1) for i in range(shards * groups - 1)]
        halo = shift(tail, ("seq", "head"), flat)
        behind = shift(tail, "seq", ahead)
        swapped = me_head
    else:
        gathered = lax.all_gather(tokens, "head", axis=0, tiled=True)
        rows = gathered.shape[0] // 2
        early, late = gathered[:rows], gathered[rows:]
        halo = behind = shift(late[rows - HALO :], "seq", ahead)
        head, tail = early[:HALO], early[rows - HALO :]
        swapped = jnp.zeros((), jnp.int32)

    gain = norm_gain.reshape(1, columns)
    pair_shape = (heads, 2 * dim, dim)
    kept = heads // 2 if heads % 2 == 0 else heads
    kept_shape = (kept,) + pair_shape[1:]
    levels = shards.bit_length() - 1
    bits = [((me_seq >> level) & 1).astype(jnp.int32).reshape(1) for level in range(levels)]
    flags = jnp.concatenate([swapped.astype(jnp.int32).reshape(1), bits[0]])
    weights = [w_query, w_key, w_value, w_beta.T, conv_weight]
    pair0, look0 = call(
        early_kernel,
        [(pair_shape, F32), ((heads, rows, 2 * dim), F32)],
        [early] + weights,
        scalars=[beta_bias],
        scratch=[pltpu.VMEM((3, rows + HALO, columns), F32)],
        grant=24,
    )
    keep, send, *held = call(
        late_kernel,
        [
            (kept_shape, BF16),
            (kept_shape, BF16),
            ((heads, rows), F32),
            ((heads, rows, 6 * dim), BF16),
            ((heads, HALO, 2 * dim), F32),
        ],
        [late] + weights + [head, tail, halo, behind, pair0],
        scalars=[flags, beta_bias],
        scratch=[pltpu.VMEM((3, rows + 3 * HALO, columns), F32)],
        grant=24,
    )
    own = keep
    for level in range(levels):
        partner = [(i, i ^ (1 << level)) for i in range(shards)]
        if level == levels - 1:
            partner = [(i, j) for i, j in partner if j > i]
        came = shift(send, "seq", partner)
        if level == 1:
            both = call(
                functools.partial(look_kernel, conv_weight.shape[1]),
                [((2, heads, rows, 2 * dim), F32)],
                held + [look0],
                scalars=[flags],
            )[0]
            came, path, both = together(came, path, both)
            if groups == 2:
                part = call(
                    half_kernel,
                    [((w_out.shape[0] // 2, width), BF16)],
                    [w_out],
                    scalars=[bits[0]],
                )[0]
        elif level > 1:
            came, path = together(came, path)
        if level == levels - 1:
            break
        send = call(
            join_kernel,
            [((kept, dim if level == levels - 2 else 2 * dim, dim), BF16)],
            [own, came],
            scalars=[bits[level]],
        )[0]
        if level == 0:
            own, came, send = together(own, came, send)
            path = call(
                open_kernel, [((kept, 2 * dim, 2 * dim), F32)], [own, came], scalars=[bits[0]]
            )[0]
        else:
            path, came, send = together(path, came, send)
            path = call(
                path_kernel, [((kept, 2 * dim, 2 * dim), F32)], [path, came], scalars=[bits[level]]
            )[0]
            if level == 1 and groups == 2:
                part, path = together(part, path)
                part = shift(part, "head", swap)
        own = send
    keep, send = call(
        enter_kernel,
        [((kept, dim, dim), BF16)] * 2,
        [came, path],
        scalars=[jnp.concatenate([bits[0], bits[levels - 1]])],
    )
    came = shift(send, "seq", [(i, i ^ 1) for i in range(shards)]) if kept < heads else send
    gone = call(
        functools.partial(finish_kernel, 1),
        [((rows, columns), BF16)],
        [keep, came, both, gain],
        scalars=[bits[0]],
    )[0]
    if groups == 2:
        theirs = shift(gone, "head", swap)
        mine = call(
            finish_mine_kernel,
            [((rows, width), BF16)],
            [keep, came, both, gain, w_out],
            scalars=[bits[0]],
            scratch=[pltpu.VMEM((rows, columns), BF16)],
        )[0]
        part, gone = together(part, gone)
        rest = shift(part, "seq", [(i, i ^ 1) for i in range(shards)])
        return call(
            output_kernel,
            [((rows, width), BF16)],
            [theirs, part, rest, mine],
            scalars=[bits[0]],
        )[0]
    normed = call(
        functools.partial(finish_kernel, 0),
        [((rows, columns), BF16)],
        [keep, came, both, gain],
        scalars=[bits[0]],
    )[0]
    product = jnp.dot(
        jnp.concatenate([normed, gone], 0), w_out, preferred_element_type=F32
    ).astype(BF16)
    return lax.psum_scatter(product, "head", scatter_dimension=0, tiled=True)


def solution(mesh):
    in_specs = (
        P(("seq", "head"), None),
        P(None, "head"),
        P(None, "head"),
        P(None, "head"),
        P(None, "head"),
        P("head"),
        P(None, None, "head"),
        P("head"),
        P("head", None),
    )
    out_specs = P(("seq", "head"), None)
    return jax.shard_map(local, mesh=mesh, in_specs=in_specs, out_specs=out_specs, check_vma=False)
```

```python
import functools

import jax
import jax.numpy as jnp
from jax import lax
from jax.experimental import pallas as pl
from jax.experimental.pallas import tpu as pltpu
from jax.sharding import PartitionSpec as P

BASE = 16
HALO = 16
F32 = jnp.float32
BF16 = jnp.bfloat16
VMEM = pl.BlockSpec(memory_space=pltpu.VMEM)
NN = ((1,), (0,))
NT = ((1,), (1,))
TN = ((0,), (0,))


def dot(left, right, dims=NN):
    return lax.dot_general(left, right, (dims, ((), ())), preferred_element_type=F32)


def split(wide):
    top = wide.astype(BF16)
    return top, (wide - top.astype(F32)).astype(BF16)


def dot_wide(left, right, dims=NN):
    left_top, left_rest = split(left)
    right_top, right_rest = split(right)
    return (
        dot(left_top, right_top, dims)
        + dot(left_rest, right_top, dims)
        + dot(left_top, right_rest, dims)
    )


def dot_half(left, right, dims=NN):
    left_top, left_rest = split(left)
    return dot(left_top, right, dims) + dot(left_rest, right, dims)


def substitute(windows):
    lanes = windows[0].shape[0]
    row = lax.broadcasted_iota(jnp.int32, (8, lanes), 0)
    lane = lax.broadcasted_iota(jnp.int32, (8, lanes), 1)
    group = lane // BASE
    bands = BASE // 8
    packed, solved = [], []
    for window in windows:
        rows = []
        for band in range(bands):
            piece = window[band * 8 : band * 8 + 8]
            for index in range(1, lanes // BASE):
                start = index * BASE + band * 8
                piece = jnp.where(group == index, window[start : start + 8], piece)
            rows.append(piece)
        packed.append(rows)
        solved.append(
            [(row + band * 8 == lane - group * BASE).astype(F32) for band in range(bands)]
        )
    for step in range(BASE - 1):
        at = step // 8
        place = group * BASE + step
        for rows, found in zip(packed, solved):
            pivot = found[at][step % 8 : step % 8 + 1]
            for band in range(at, bands):
                if band > at or step % 8 < 7:
                    column = jnp.take_along_axis(rows[band], place, axis=1)
                    found[band] = found[band] - column * pivot
    return [
        jnp.concatenate(
            [jnp.where(group == index, piece, 0.0) for index in range(lanes // BASE) for piece in found],
            0,
        )
        for found in solved
    ]


def invert(lowers):
    size = lowers[0].shape[0]
    lanes = 128
    starts = range(0, size, lanes)
    windows = [low[at : at + lanes, at : at + lanes] for low in lowers for at in starts]
    inverses = substitute(windows)
    row = lax.broadcasted_iota(jnp.int32, (lanes, lanes), 0)
    lane = lax.broadcasted_iota(jnp.int32, (lanes, lanes), 1)
    width = BASE
    while width < lanes:
        mask = (row // (2 * width) == lane // (2 * width)) & (row // width != lane // width)
        picks = range(width, lanes, 2 * width)

        def odd(full):
            return jnp.concatenate([full[at : at + width] for at in picks], 0)

        def spread(picked):
            none = jnp.zeros((width, lanes), F32)
            return jnp.concatenate(
                [
                    each
                    for index in range(len(picks))
                    for each in (none, picked[index * width : (index + 1) * width])
                ],
                0,
            )

        inner = [
            dot_wide(odd(jnp.where(mask, window, 0.0)), inverse)
            for window, inverse in zip(windows, inverses)
        ]
        inverses = [
            inverse - spread(dot_wide(odd(inverse), spread(each)))
            for inverse, each in zip(inverses, inner)
        ]
        width *= 2
    count = len(starts)
    groups = [inverses[at : at + count] for at in range(0, len(inverses), count)]
    while width < size:
        joined = []
        below = [
            [
                dot_wide(
                    low[(at + 1) * width : (at + 2) * width, at * width : (at + 1) * width], parts[at]
                )
                for at in range(0, len(parts), 2)
            ]
            for low, parts in zip(lowers, groups)
        ]
        for inner, parts in zip(below, groups):
            merged = []
            for at in range(0, len(parts), 2):
                first, second = parts[at], parts[at + 1]
                corner = -dot_wide(second, inner[at // 2])
                merged.append(
                    jnp.concatenate(
                        [
                            jnp.concatenate([first, jnp.zeros_like(first)], 1),
                            jnp.concatenate([corner, second], 1),
                        ],
                        0,
                    )
                )
            joined.append(merged)
        groups = joined
        width *= 2
    return [parts[0] for parts in groups]


def activate(x, weights, conv_ref, proj_ref, blocks):
    taps = conv_ref.shape[1]
    active = [[] for _ in blocks]
    for index, w_ref in enumerate(weights):
        proj_ref[index] = dot(x, w_ref[...]).astype(BF16).astype(F32)
        for (start, rows), outs in zip(blocks, active):
            first = start - (taps - 1)
            total = proj_ref[index, first : first + rows] * conv_ref[index, 0:1]
            for tap in range(1, taps):
                total = total + proj_ref[index, first + tap : first + tap + rows] * conv_ref[
                    index, tap : tap + 1
                ]
            outs.append((total / (1.0 + jnp.exp(-total))).astype(BF16))
    return active


def invert_few(count, lowers):
    inverses = []
    for lower in lowers:
        eye = jnp.eye(lower.shape[0], dtype=F32)
        inverse = eye - lower
        for _ in range(count - 2):
            inverse = eye - dot_wide(lower, inverse)
        inverses.append(inverse)
    return inverses


def transitions(keys, values, rates, invert=invert):
    rows, dim = keys[0].shape
    row = lax.broadcasted_iota(jnp.int32, (rows, rows), 0)
    lane = lax.broadcasted_iota(jnp.int32, (rows, rows), 1)
    norms, norm_rows, rate_rows, lowers = [], [], [], []
    for key, rate_row in zip(keys, rates):
        rate = jnp.sum(jnp.where(row == lane, rate_row, 0.0), 1, keepdims=True)
        wide_key = key.astype(F32)
        norm = lax.rsqrt(jnp.sum(wide_key * wide_key, 1, keepdims=True) + 1e-6)
        norm_row = jnp.sum(jnp.where(row == lane, norm, 0.0), 0, keepdims=True)
        norms.append(norm)
        norm_rows.append(norm_row)
        rate_rows.append(rate_row)
        gram = dot(key, key, NT)
        lowers.append(jnp.where(row > lane, gram * (rate * norm) * norm_row, 0.0))
    inverses = [each * rate for each, rate in zip(invert(lowers), rate_rows)]
    eye = jnp.eye(dim, dtype=F32)
    solved = []
    for key, value, inverse, norm_row in zip(keys, values, inverses, norm_rows):
        fresh = dot_half(inverse, value)
        weight = dot_half(inverse * norm_row, key)
        solved.append(jnp.concatenate([weight, fresh], 1))
    pairs = []
    for key, each, norm in zip(keys, solved, norms):
        top, rest = split(each * norm)
        moved = dot(key, top, TN) + dot(key, rest, TN)
        pairs.append(jnp.concatenate([eye - moved[:, :dim], moved[:, dim:]], 1))
    return pairs, solved, norm_rows


def look(query, key, norm_row, solved):
    rows, dim = query.shape
    row = lax.broadcasted_iota(jnp.int32, (rows, rows), 0)
    lane = lax.broadcasted_iota(jnp.int32, (rows, rows), 1)
    attend = jnp.where(row >= lane, dot(query, key, NT) * norm_row, 0.0)
    seen = dot_half(attend, solved)
    return jnp.concatenate([query.astype(F32) - seen[:, :dim], seen[:, dim:]], 1)


def spans_of(count, width):
    dim = width // count
    return [slice(head * dim, (head + 1) * dim) for head in range(count)]


def write_rates(x, wb, bias_ref):
    logits = dot(wb, x, NT)
    return [
        2.0 / (1.0 + jnp.exp(-(logits[head : head + 1] + bias_ref[head])))
        for head in range(wb.shape[0])
    ]


def edge_kernel(x_ref, head_ref, tail_ref):
    head_ref[...] = x_ref[: head_ref.shape[0]]
    tail_ref[...] = x_ref[x_ref.shape[0] - tail_ref.shape[0] :]


def early_kernel(
    bias_ref, x_ref, wq_ref, wk_ref, wv_ref, wb_ref, conv_ref, pair_ref, look_ref, proj_ref
):
    rows, width = x_ref.shape
    x = jnp.concatenate([jnp.zeros((HALO, width), BF16), x_ref[...]], 0)
    active = activate(x, (wq_ref, wk_ref, wv_ref), conv_ref, proj_ref, [(HALO, rows)])[0]
    spans = spans_of(pair_ref.shape[0], active[0].shape[1])
    queries, keys, values = ([each[:, span] for span in spans] for each in active)
    lane = lax.broadcasted_iota(jnp.int32, (1, rows), 1)
    rates = [
        jnp.where(lane < conv_ref.shape[1] - 1, 0.0, each)
        for each in write_rates(x_ref[...], wb_ref[...], bias_ref)
    ]
    pairs, solved, norm_rows = transitions(keys, values, rates)
    for head in range(len(spans)):
        pair_ref[head] = pairs[head]
        look_ref[head] = look(
            queries[head], keys[head], norm_rows[head], solved[head].astype(BF16)
        )


def late_kernel(
    flags_ref,
    bias_ref,
    x_ref,
    wq_ref,
    wk_ref,
    wv_ref,
    wb_ref,
    conv_ref,
    head_ref,
    tail_ref,
    halo_ref,
    behind_ref,
    early_ref,
    keep_ref,
    send_ref,
    norm_ref,
    held_ref,
    mini_ref,
    proj_ref,
):
    heads = early_ref.shape[0]
    kept = keep_ref.shape[0]
    rows = x_ref.shape[0]
    swapped = flags_ref[0] == 1
    halo = jnp.where(swapped, behind_ref[...], tail_ref[...])
    x = jnp.concatenate([halo, x_ref[...], halo_ref[...], head_ref[...]], 0)
    active, few = activate(
        x,
        (wq_ref, wk_ref, wv_ref),
        conv_ref,
        proj_ref,
        [(HALO, rows), (2 * HALO + rows, HALO)],
    )
    spans = spans_of(heads, active[0].shape[1])
    queries, keys, values = ([each[:, span] for span in spans] for each in active)
    rates = write_rates(x_ref[...], wb_ref[...], bias_ref)
    lane = lax.broadcasted_iota(jnp.int32, (1, HALO), 1)
    few_rates = [
        jnp.where(lane < conv_ref.shape[1] - 1, each, 0.0)
        for each in write_rates(head_ref[...], wb_ref[...], bias_ref)
    ]
    few_queries, few_keys, few_values = ([each[:, span] for span in spans] for each in few)
    few_pairs, few_solved, few_norm_rows = transitions(
        few_keys, few_values, few_rates, functools.partial(invert_few, conv_ref.shape[1] - 1)
    )
    early = []
    for head in range(heads):
        mini_ref[head] = look(
            few_queries[head], few_keys[head], few_norm_rows[head], few_solved[head].astype(BF16)
        )
        early.append(compose(few_pairs[head], early_ref[head]))
    pairs, solved, norm_rows = transitions(keys, values, rates)
    bit = flags_ref[1]
    wholes = []
    for head, late in enumerate(pairs):
        norm_ref[head : head + 1] = norm_rows[head]
        low = jnp.where(swapped, late, early[head])
        held_ref[head] = jnp.concatenate(
            [
                solved[head].astype(BF16),
                jnp.concatenate([queries[head], keys[head]], 1),
                low.astype(BF16),
                few_pairs[head].astype(BF16),
            ],
            0,
        )
        wholes.append(compose(low, jnp.where(swapped, early[head], late)).astype(BF16))
    for head in range(kept):
        if kept == heads:
            keep_ref[head] = wholes[head]
            send_ref[head] = wholes[head]
        else:
            one, two = wholes[head], wholes[head + kept]
            keep_ref[head] = jnp.where(bit == 1, two, one)
            send_ref[head] = jnp.where(bit == 1, one, two)


def after(reads, pair):
    dim = pair.shape[0]
    through = dot(reads[:, :dim].astype(BF16), pair)
    return jnp.concatenate([through[:, :dim], through[:, dim:] + reads[:, dim:]], 1)


def look_kernel(taps, flags_ref, norm_ref, held_ref, mini_ref, early_ref, both_ref):
    swapped = flags_ref[0] == 1
    heads = held_ref.shape[0]
    dim = held_ref.shape[2] // 2
    rows = (held_ref.shape[1] - 2 * dim) // 2
    row = lax.broadcasted_iota(jnp.int32, (HALO, 2 * dim), 0)
    for head in range(heads):
        late = look(
            held_ref[head, rows : 2 * rows, :dim],
            held_ref[head, rows : 2 * rows, dim:],
            norm_ref[head : head + 1],
            held_ref[head, :rows],
        )
        first = held_ref[head, 2 * rows : 2 * rows + dim]
        early = after(early_ref[head], held_ref[head, 2 * rows + dim :])
        top = jnp.where(row < taps - 1, mini_ref[head], early[:HALO])
        early = jnp.concatenate([top, early[HALO:]], 0)
        later = after(jnp.where(swapped, early, late), first)
        both_ref[0, head] = jnp.where(swapped, later, early)
        both_ref[1, head] = jnp.where(swapped, late, later)


def compose(low, high):
    dim = low.shape[0]
    joined = dot_wide(high[:, :dim], low)
    return jnp.concatenate([joined[:, :dim], joined[:, dim:] + high[:, dim:]], 1)


def join_kernel(flags_ref, own_ref, other_ref, send_ref):
    later = flags_ref[0] == 1
    for head in range(own_ref.shape[0]):
        own, other = own_ref[head], other_ref[head]
        low = jnp.where(later, other, own)
        high = jnp.where(later, own, other)
        dim = low.shape[0]
        landed = send_ref.shape[2] - dim
        joined = dot(high[:, :dim], low)
        if landed > 0:
            send_ref[head, :, :dim] = joined[:, :dim].astype(BF16)
        send_ref[head, :, landed:] = (joined[:, dim:] + high[:, dim:].astype(F32)).astype(BF16)


def open_kernel(flags_ref, own_ref, other_ref, path_ref):
    dim = own_ref.shape[1]
    row = lax.broadcasted_iota(jnp.int32, (dim, 2 * dim), 0)
    lane = lax.broadcasted_iota(jnp.int32, (dim, 2 * dim), 1)
    for head in range(own_ref.shape[0]):
        path_ref[head, :dim] = (row == lane).astype(F32)
        low = jnp.where(flags_ref[0] == 1, other_ref[head], own_ref[head])
        path_ref[head, dim:] = low.astype(F32)


def path_kernel(flags_ref, path_ref, came_ref, out_ref):
    dim = came_ref.shape[1]
    for head in range(came_ref.shape[0]):
        path = path_ref[head]
        through = dot_half(path[:, :dim], came_ref[head])
        longer = jnp.concatenate([through[:, :dim], through[:, dim:] + path[:, dim:]], 1)
        out_ref[head] = jnp.where(flags_ref[0] == 1, longer, path)


def enter_kernel(flags_ref, state_ref, path_ref, keep_ref, send_ref):
    dim = state_ref.shape[1]
    for head in range(keep_ref.shape[0]):
        state = jnp.where(flags_ref[1] == 1, state_ref[head], jnp.zeros_like(state_ref[head]))
        path = path_ref[head]
        both = (dot(path[:, :dim].astype(BF16), state) + path[:, dim:]).astype(BF16)
        later = flags_ref[0] == 1
        keep_ref[head] = jnp.where(later, both[dim:], both[:dim])
        send_ref[head] = jnp.where(later, both[:dim], both[dim:])


def finish_kernel(place, flags_ref, keep_ref, came_ref, both_ref, gain_ref, out_ref):
    count, dim = keep_ref.shape[:2]
    heads = both_ref.shape[1]
    for head, span in enumerate(spans_of(heads, heads * dim)):
        state = keep_ref[head % count]
        if count < heads:
            state = jnp.where(flags_ref[0] == head // count, state, came_ref[head % count])
        reach = both_ref[place, head, :, :dim].astype(BF16)
        rows = both_ref[place, head, :, dim:] + dot(reach, state)
        scale = lax.rsqrt(jnp.mean(rows * rows, 1, keepdims=True) + 1e-5)
        out_ref[:, span] = (rows * scale * gain_ref[:, span]).astype(BF16)


def finish_mine_kernel(flags_ref, keep_ref, came_ref, both_ref, gain_ref, w_ref, out_ref, normed_ref):
    finish_kernel(0, flags_ref, keep_ref, came_ref, both_ref, gain_ref, normed_ref)
    out_ref[...] = dot(normed_ref[...], w_ref[...]).astype(BF16)


def hold_kernel(w_ref, held_ref):
    held_ref[...] = w_ref[...]


def output_kernel(theirs_ref, w_ref, mine_ref, out_ref):
    theirs = dot(theirs_ref[...], w_ref[...]).astype(BF16).astype(F32)
    out_ref[...] = (mine_ref[...].astype(F32) + theirs).astype(BF16)


def call(kernel, outs, inputs, scalars=(), scratch=(), flops=10**7, moved=10**5, grant=8):
    specs = [pl.BlockSpec(memory_space=pltpu.SMEM)] * len(scalars)
    specs += [VMEM] * len(inputs)
    return pl.pallas_call(
        kernel,
        out_shape=[jax.ShapeDtypeStruct(shape, dtype) for shape, dtype in outs],
        in_specs=specs,
        out_specs=[VMEM] * len(outs),
        scratch_shapes=list(scratch),
        compiler_params=pltpu.CompilerParams(vmem_limit_bytes=grant * 1024 * 1024),
        cost_estimate=pl.CostEstimate(flops=flops, bytes_accessed=moved, transcendentals=0),
    )(*scalars, *inputs)


def together(*arrays):
    return lax.optimization_barrier(arrays)


def shift(block, axes, pairs):
    return lax.ppermute(block, axes, pairs)


def local(tokens, w_query, w_key, w_value, w_beta, beta_bias, conv_weight, norm_gain, w_out):
    groups = lax.axis_size("head")
    shards = lax.axis_size("seq")
    heads = beta_bias.shape[0]
    columns = w_query.shape[1]
    dim = columns // heads
    width = tokens.shape[1]
    me_head = lax.axis_index("head")
    me_seq = lax.axis_index("seq")
    ahead = [(i, i + 1) for i in range(shards - 1)]

    if groups == 2:
        rows = tokens.shape[0]
        swap = [(0, 1), (1, 0)]
        early = tokens
        late = shift(tokens, "head", swap)
        head, tail = call(
            edge_kernel, [((HALO, width), BF16)] * 2, [tokens], flops=2 * 10**10, moved=10**6
        )
        flat = [(i, i + 1) for i in range(shards * groups - 1)]
        halo = shift(tail, ("seq", "head"), flat)
        behind = shift(tail, "seq", ahead)
        swapped = me_head
    else:
        gathered = lax.all_gather(tokens, "head", axis=0, tiled=True)
        rows = gathered.shape[0] // 2
        early, late = gathered[:rows], gathered[rows:]
        halo = behind = shift(late[rows - HALO :], "seq", ahead)
        head, tail = early[:HALO], early[rows - HALO :]
        swapped = jnp.zeros((), jnp.int32)

    gain = norm_gain.reshape(1, columns)
    pair_shape = (heads, dim, 2 * dim)
    kept = heads // 2 if heads % 2 == 0 else heads
    kept_shape = (kept,) + pair_shape[1:]
    levels = shards.bit_length() - 1
    bits = [((me_seq >> level) & 1).astype(jnp.int32).reshape(1) for level in range(levels)]
    flags = jnp.concatenate([swapped.astype(jnp.int32).reshape(1), bits[0]])
    weights = [w_query, w_key, w_value, w_beta.T, conv_weight]
    pair0, look0 = call(
        early_kernel,
        [(pair_shape, F32), ((heads, rows, 2 * dim), F32)],
        [early] + weights,
        scalars=[beta_bias],
        scratch=[pltpu.VMEM((3, rows + HALO, columns), F32)],
        grant=24,
    )
    keep, send, *held = call(
        late_kernel,
        [
            (kept_shape, BF16),
            (kept_shape, BF16),
            ((heads, rows), F32),
            ((heads, 2 * rows + 2 * dim, 2 * dim), BF16),
            ((heads, HALO, 2 * dim), F32),
        ],
        [late] + weights + [head, tail, halo, behind, pair0],
        scalars=[flags, beta_bias],
        scratch=[pltpu.VMEM((3, rows + 3 * HALO, columns), F32)],
        grant=24,
    )
    if groups == 2:
        w_sent, keep = together(w_out, keep)
        w_other = shift(w_sent, "head", swap)
    own = keep
    for level in range(levels):
        partner = [(i, i ^ (1 << level)) for i in range(shards)]
        if level == levels - 1:
            partner = [(i, j) for i, j in partner if j > i]
        came = shift(send, "seq", partner)
        if level == 1:
            both = call(
                functools.partial(look_kernel, conv_weight.shape[1]),
                [((2, heads, rows, 2 * dim), F32)],
                held + [look0],
                scalars=[flags],
            )[0]
            came, path, both = together(came, path, both)
        elif level > 1:
            came, path = together(came, path)
        if level == levels - 1:
            break
        send = call(
            join_kernel,
            [((kept, dim, dim if level == levels - 2 else 2 * dim), BF16)],
            [own, came],
            scalars=[bits[level]],
        )[0]
        if level == 0:
            own, came, send = together(own, came, send)
            path = call(
                open_kernel, [((kept, 2 * dim, 2 * dim), F32)], [own, came], scalars=[bits[0]]
            )[0]
        else:
            path, came, send = together(path, came, send)
            path = call(
                path_kernel, [((kept, 2 * dim, 2 * dim), F32)], [path, came], scalars=[bits[level]]
            )[0]
        own = send
    keep, send = call(
        enter_kernel,
        [((kept, dim, dim), BF16)] * 2,
        [came, path],
        scalars=[jnp.concatenate([bits[0], bits[levels - 1]])],
    )
    came = shift(send, "seq", [(i, i ^ 1) for i in range(shards)]) if kept < heads else send
    gone = call(
        functools.partial(finish_kernel, 1),
        [((rows, columns), BF16)],
        [keep, came, both, gain],
        scalars=[bits[0]],
    )[0]
    if groups == 2:
        theirs = shift(gone, "head", swap)
        mine = call(
            finish_mine_kernel,
            [((rows, width), BF16)],
            [keep, came, both, gain, w_out],
            scalars=[bits[0]],
            scratch=[pltpu.VMEM((rows, columns), BF16)],
        )[0]
        w_other, gone = together(w_other, gone)
        whole = call(hold_kernel, [(w_out.shape, BF16)], [w_other])[0]
        theirs, whole = together(theirs, whole)
        return call(output_kernel, [((rows, width), BF16)], [theirs, whole, mine])[0]
    normed = call(
        functools.partial(finish_kernel, 0),
        [((rows, columns), BF16)],
        [keep, came, both, gain],
        scalars=[bits[0]],
    )[0]
    product = jnp.dot(
        jnp.concatenate([normed, gone], 0), w_out, preferred_element_type=F32
    ).astype(BF16)
    return lax.psum_scatter(product, "head", scatter_dimension=0, tiled=True)


def solution(mesh):
    in_specs = (
        P(("seq", "head"), None),
        P(None, "head"),
        P(None, "head"),
        P(None, "head"),
        P(None, "head"),
        P("head"),
        P(None, None, "head"),
        P("head"),
        P("head", None),
    )
    out_specs = P(("seq", "head"), None)
    return jax.shard_map(local, mesh=mesh, in_specs=in_specs, out_specs=out_specs, check_vma=False)
```

```python
import functools

import jax
import jax.numpy as jnp
from jax import lax
from jax.experimental import pallas as pl
from jax.experimental.pallas import tpu as pltpu
from jax.sharding import PartitionSpec as P

BASE = 16
HALO = 16
F32 = jnp.float32
BF16 = jnp.bfloat16
VMEM = pl.BlockSpec(memory_space=pltpu.VMEM)
NN = ((1,), (0,))
NT = ((1,), (1,))
TN = ((0,), (0,))


def dot(left, right, dims=NN):
    return lax.dot_general(left, right, (dims, ((), ())), preferred_element_type=F32)


def split(wide):
    top = wide.astype(BF16)
    return top, (wide - top.astype(F32)).astype(BF16)


def dot_wide(left, right, dims=NN):
    left_top, left_rest = split(left)
    right_top, right_rest = split(right)
    return (
        dot(left_top, right_top, dims)
        + dot(left_rest, right_top, dims)
        + dot(left_top, right_rest, dims)
    )


def dot_half(left, right, dims=NN):
    left_top, left_rest = split(left)
    return dot(left_top, right, dims) + dot(left_rest, right, dims)


def substitute(windows):
    lanes = windows[0].shape[0]
    row = lax.broadcasted_iota(jnp.int32, (8, lanes), 0)
    lane = lax.broadcasted_iota(jnp.int32, (8, lanes), 1)
    group = lane // BASE
    bands = BASE // 8
    packed, solved = [], []
    for window in windows:
        rows = []
        for band in range(bands):
            piece = window[band * 8 : band * 8 + 8]
            for index in range(1, lanes // BASE):
                start = index * BASE + band * 8
                piece = jnp.where(group == index, window[start : start + 8], piece)
            rows.append(piece)
        packed.append(rows)
        solved.append(
            [(row + band * 8 == lane - group * BASE).astype(F32) for band in range(bands)]
        )
    for step in range(BASE - 1):
        at = step // 8
        place = group * BASE + step
        for rows, found in zip(packed, solved):
            pivot = found[at][step % 8 : step % 8 + 1]
            for band in range(at, bands):
                if band > at or step % 8 < 7:
                    column = jnp.take_along_axis(rows[band], place, axis=1)
                    found[band] = found[band] - column * pivot
    return [
        jnp.concatenate(
            [jnp.where(group == index, piece, 0.0) for index in range(lanes // BASE) for piece in found],
            0,
        )
        for found in solved
    ]


def invert(lowers):
    size = lowers[0].shape[0]
    lanes = 128
    starts = range(0, size, lanes)
    windows = [low[at : at + lanes, at : at + lanes] for low in lowers for at in starts]
    inverses = substitute(windows)
    row = lax.broadcasted_iota(jnp.int32, (lanes, lanes), 0)
    lane = lax.broadcasted_iota(jnp.int32, (lanes, lanes), 1)
    width = BASE
    while width < lanes:
        mask = (row // (2 * width) == lane // (2 * width)) & (row // width != lane // width)
        picks = range(width, lanes, 2 * width)

        def odd(full):
            return jnp.concatenate([full[at : at + width] for at in picks], 0)

        def spread(picked):
            none = jnp.zeros((width, lanes), F32)
            return jnp.concatenate(
                [
                    each
                    for index in range(len(picks))
                    for each in (none, picked[index * width : (index + 1) * width])
                ],
                0,
            )

        inner = [
            dot_wide(odd(jnp.where(mask, window, 0.0)), inverse)
            for window, inverse in zip(windows, inverses)
        ]
        inverses = [
            inverse - spread(dot_wide(odd(inverse), spread(each)))
            for inverse, each in zip(inverses, inner)
        ]
        width *= 2
    count = len(starts)
    groups = [inverses[at : at + count] for at in range(0, len(inverses), count)]
    while width < size:
        joined = []
        below = [
            [
                dot_wide(
                    low[(at + 1) * width : (at + 2) * width, at * width : (at + 1) * width], parts[at]
                )
                for at in range(0, len(parts), 2)
            ]
            for low, parts in zip(lowers, groups)
        ]
        for inner, parts in zip(below, groups):
            merged = []
            for at in range(0, len(parts), 2):
                first, second = parts[at], parts[at + 1]
                corner = -dot_wide(second, inner[at // 2])
                merged.append(
                    jnp.concatenate(
                        [
                            jnp.concatenate([first, jnp.zeros_like(first)], 1),
                            jnp.concatenate([corner, second], 1),
                        ],
                        0,
                    )
                )
            joined.append(merged)
        groups = joined
        width *= 2
    return [parts[0] for parts in groups]


def activate(x, weights, conv_ref, proj_ref, blocks):
    taps = conv_ref.shape[1]
    active = [[] for _ in blocks]
    for index, w_ref in enumerate(weights):
        proj_ref[index] = dot(x, w_ref[...]).astype(BF16).astype(F32)
        for (start, rows), outs in zip(blocks, active):
            first = start - (taps - 1)
            total = proj_ref[index, first : first + rows] * conv_ref[index, 0:1]
            for tap in range(1, taps):
                total = total + proj_ref[index, first + tap : first + tap + rows] * conv_ref[
                    index, tap : tap + 1
                ]
            outs.append((total / (1.0 + jnp.exp(-total))).astype(BF16))
    return active


def invert_few(count, lowers):
    inverses = []
    for lower in lowers:
        eye = jnp.eye(lower.shape[0], dtype=F32)
        inverse = eye - lower
        for _ in range(count - 2):
            inverse = eye - dot_wide(lower, inverse)
        inverses.append(inverse)
    return inverses


def within(shape, group):
    row = lax.broadcasted_iota(jnp.int32, shape, 0)
    lane = lax.broadcasted_iota(jnp.int32, shape, 1)
    if group is None or group >= shape[0]:
        return row, lane, True
    return row, lane, row // group == lane // group


def solve(keys, values, rates, invert=invert, group=None):
    rows, dim = keys[0].shape
    row, lane, same = within((rows, rows), group)
    norms, norm_rows, lowers = [], [], []
    for key, rate_row in zip(keys, rates):
        rate = jnp.sum(jnp.where(row == lane, rate_row, 0.0), 1, keepdims=True)
        wide_key = key.astype(F32)
        norm = lax.rsqrt(jnp.sum(wide_key * wide_key, 1, keepdims=True) + 1e-6)
        norm_row = jnp.sum(jnp.where(row == lane, norm, 0.0), 0, keepdims=True)
        norms.append(norm)
        norm_rows.append(norm_row)
        gram = dot(key, key, NT)
        lowers.append(jnp.where((row > lane) & same, gram * (rate * norm) * norm_row, 0.0))
    solved = []
    for key, value, inverse, rate_row, norm in zip(keys, values, invert(lowers), rates, norms):
        top, rest = split(inverse * rate_row)
        unit, unit_rest = split(key.astype(F32) * norm)
        both = jnp.concatenate([unit, value], 1)
        each = dot(top, both) + dot(rest, both)
        solved.append(jnp.concatenate([each[:, :dim] + dot(top, unit_rest), each[:, dim:]], 1))
    return solved, norms, norm_rows


def pair_of(key, solved, norm):
    dim = key.shape[1]
    top, rest = split(solved * norm)
    moved = dot(key, top, TN) + dot(key, rest, TN)
    return jnp.concatenate([jnp.eye(dim, dtype=F32) - moved[:, :dim], moved[:, dim:]], 1)


def transitions(keys, values, rates):
    solved, norms, norm_rows = solve(keys, values, rates)
    return [pair_of(*each) for each in zip(keys, solved, norms)], solved, norm_rows


def look(query, key, norm_row, solved, group=None):
    rows, dim = query.shape
    row, lane, same = within((rows, rows), group)
    attend = jnp.where((row >= lane) & same, dot(query, key, NT) * norm_row, 0.0)
    seen = dot_half(attend, solved)
    return jnp.concatenate([query.astype(F32) - seen[:, :dim], seen[:, dim:]], 1)


def spans_of(count, width):
    dim = width // count
    return [slice(head * dim, (head + 1) * dim) for head in range(count)]


def write_rates(x, wb, bias_ref):
    logits = dot(wb, x, NT)
    return [
        2.0 / (1.0 + jnp.exp(-(logits[head : head + 1] + bias_ref[head])))
        for head in range(wb.shape[0])
    ]


def edge_kernel(x_ref, head_ref, tail_ref):
    head_ref[...] = x_ref[: head_ref.shape[0]]
    tail_ref[...] = x_ref[x_ref.shape[0] - tail_ref.shape[0] :]


def early_kernel(
    bias_ref, x_ref, wq_ref, wk_ref, wv_ref, wb_ref, conv_ref, pair_ref, look_ref, proj_ref
):
    rows, width = x_ref.shape
    x = jnp.concatenate([jnp.zeros((HALO, width), BF16), x_ref[...]], 0)
    active = activate(x, (wq_ref, wk_ref, wv_ref), conv_ref, proj_ref, [(HALO, rows)])[0]
    spans = spans_of(pair_ref.shape[0], active[0].shape[1])
    queries, keys, values = ([each[:, span] for span in spans] for each in active)
    lane = lax.broadcasted_iota(jnp.int32, (1, rows), 1)
    rates = [
        jnp.where(lane < conv_ref.shape[1] - 1, 0.0, each)
        for each in write_rates(x_ref[...], wb_ref[...], bias_ref)
    ]
    pairs, solved, norm_rows = transitions(keys, values, rates)
    for head in range(len(spans)):
        pair_ref[head] = pairs[head]
        look_ref[head] = look(
            queries[head], keys[head], norm_rows[head], solved[head].astype(BF16)
        ).astype(BF16)


def late_kernel(
    swapped_ref,
    bit_ref,
    bias_ref,
    x_ref,
    wq_ref,
    wk_ref,
    wv_ref,
    wb_ref,
    conv_ref,
    head_ref,
    tail_ref,
    halo_ref,
    behind_ref,
    early_ref,
    keep_ref,
    send_ref,
    norm_ref,
    held_ref,
    proj_ref,
):
    heads = early_ref.shape[0]
    kept = keep_ref.shape[0]
    rows = x_ref.shape[0]
    swapped = swapped_ref[0] == 1
    halo = jnp.where(swapped, behind_ref[...], tail_ref[...])
    x = jnp.concatenate([halo, x_ref[...], halo_ref[...], head_ref[...]], 0)
    active, few = activate(
        x,
        (wq_ref, wk_ref, wv_ref),
        conv_ref,
        proj_ref,
        [(HALO, rows), (2 * HALO + rows, HALO)],
    )
    spans = spans_of(heads, active[0].shape[1])
    queries, keys, values = ([each[:, span] for span in spans] for each in active)
    rates = write_rates(x_ref[...], wb_ref[...], bias_ref)
    lane = lax.broadcasted_iota(jnp.int32, (1, HALO), 1)
    few_rates = jnp.concatenate(
        [
            jnp.where(lane < conv_ref.shape[1] - 1, each, 0.0)
            for each in write_rates(head_ref[...], wb_ref[...], bias_ref)
        ],
        1,
    )
    stacked = [jnp.concatenate([each[:, span] for span in spans], 0) for each in few]
    few_solved, few_norms, few_norm_row = solve(
        stacked[1:2],
        stacked[2:],
        [few_rates],
        functools.partial(invert_few, conv_ref.shape[1] - 1),
        HALO,
    )
    few_solved, few_norms = few_solved[0], few_norms[0]
    mini = look(stacked[0], stacked[1], few_norm_row[0], few_solved.astype(BF16), HALO)
    few_pairs, early = [], []
    for head in range(heads):
        at = slice(head * HALO, (head + 1) * HALO)
        few_pair = pair_of(stacked[1][at], few_solved[at], few_norms[at])
        few_pairs.append(few_pair.astype(BF16))
        early.append(compose(few_pair, early_ref[head]))
    pairs, solved, norm_rows = transitions(keys, values, rates)
    bit = bit_ref[0]
    wholes = []
    for head, late in enumerate(pairs):
        norm_ref[head : head + 1] = norm_rows[head]
        low = jnp.where(swapped, late, early[head])
        held_ref[head] = jnp.concatenate(
            [
                solved[head].astype(BF16),
                jnp.concatenate([queries[head], keys[head]], 1),
                low.astype(BF16),
                few_pairs[head],
                mini[head * HALO : (head + 1) * HALO].astype(BF16),
            ],
            0,
        )
        wholes.append(compose(low, jnp.where(swapped, early[head], late)).astype(BF16))
    for head in range(kept):
        if kept == heads:
            keep_ref[head] = wholes[head]
            send_ref[head] = wholes[head]
        else:
            one, two = wholes[head], wholes[head + kept]
            keep_ref[head] = jnp.where(bit == 1, two, one)
            send_ref[head] = jnp.where(bit == 1, one, two)


def after(reads, pair):
    dim = pair.shape[0]
    through = dot(reads[:, :dim].astype(BF16), pair)
    return jnp.concatenate([through[:, :dim], through[:, dim:] + reads[:, dim:]], 1)


def look_late_kernel(swapped_ref, norm_ref, held_ref, late_ref):
    heads = held_ref.shape[0]
    rows = norm_ref.shape[1]
    dim = held_ref.shape[2] // 2
    for head in range(heads):
        late = look(
            held_ref[head, rows : 2 * rows, :dim],
            held_ref[head, rows : 2 * rows, dim:],
            norm_ref[head : head + 1],
            held_ref[head, :rows],
        )
        later = after(late, held_ref[head, 2 * rows : 2 * rows + dim])
        late_ref[head] = jnp.where(swapped_ref[0] == 1, late, later).astype(BF16)


def look_early_kernel(taps, swapped_ref, held_ref, early_ref, out_ref):
    heads, rows, wide = early_ref.shape
    dim = wide // 2
    row = lax.broadcasted_iota(jnp.int32, (HALO, wide), 0)
    start = 2 * rows
    for head in range(heads):
        early = after(early_ref[head].astype(F32), held_ref[head, start + dim : start + 2 * dim])
        few = held_ref[head, start + 2 * dim :].astype(F32)
        top = jnp.where(row < taps - 1, few, early[:HALO])
        early = jnp.concatenate([top, early[HALO:]], 0)
        later = after(early, held_ref[head, start : start + dim])
        out_ref[head] = jnp.where(swapped_ref[0] == 1, later, early).astype(BF16)


def compose(low, high):
    dim = low.shape[0]
    joined = dot_wide(high[:, :dim], low)
    return jnp.concatenate([joined[:, :dim], joined[:, dim:] + high[:, dim:]], 1)


def join_kernel(flags_ref, own_ref, other_ref, send_ref):
    later = flags_ref[0] == 1
    for head in range(own_ref.shape[0]):
        own, other = own_ref[head], other_ref[head]
        low = jnp.where(later, other, own)
        high = jnp.where(later, own, other)
        dim = low.shape[0]
        landed = send_ref.shape[2] - dim
        joined = dot(high[:, :dim], low)
        if landed > 0:
            send_ref[head, :, :dim] = joined[:, :dim].astype(BF16)
        send_ref[head, :, landed:] = (joined[:, dim:] + high[:, dim:].astype(F32)).astype(BF16)


def open_kernel(flags_ref, own_ref, other_ref, path_ref):
    dim = own_ref.shape[1]
    row = lax.broadcasted_iota(jnp.int32, (dim, 2 * dim), 0)
    lane = lax.broadcasted_iota(jnp.int32, (dim, 2 * dim), 1)
    for head in range(own_ref.shape[0]):
        path_ref[head, :dim] = (row == lane).astype(BF16)
        low = jnp.where(flags_ref[0] == 1, other_ref[head], own_ref[head])
        path_ref[head, dim:] = low


def path_kernel(flags_ref, path_ref, came_ref, out_ref):
    dim = came_ref.shape[1]
    for head in range(came_ref.shape[0]):
        path = path_ref[head]
        through = dot(path[:, :dim], came_ref[head])
        longer = jnp.concatenate([through[:, :dim], through[:, dim:] + path[:, dim:].astype(F32)], 1)
        out_ref[head] = jnp.where(flags_ref[0] == 1, longer.astype(BF16), path)


def enter_kernel(bit_ref, reached_ref, state_ref, path_ref, keep_ref, send_ref):
    dim = state_ref.shape[1]
    for head in range(keep_ref.shape[0]):
        state = jnp.where(reached_ref[0] == 1, state_ref[head], jnp.zeros_like(state_ref[head]))
        path = path_ref[head]
        both = (dot(path[:, :dim], state) + path[:, dim:].astype(F32)).astype(BF16)
        later = bit_ref[0] == 1
        keep_ref[head] = jnp.where(later, both[dim:], both[:dim])
        send_ref[head] = jnp.where(later, both[:dim], both[dim:])


def finish_kernel(flags_ref, keep_ref, came_ref, reads_ref, gain_ref, out_ref):
    count, dim = keep_ref.shape[:2]
    heads = reads_ref.shape[0]
    for head, span in enumerate(spans_of(heads, heads * dim)):
        state = keep_ref[head % count]
        if count < heads:
            state = jnp.where(flags_ref[0] == head // count, state, came_ref[head % count])
        reach = reads_ref[head, :, :dim]
        rows = reads_ref[head, :, dim:].astype(F32) + dot(reach, state)
        scale = lax.rsqrt(jnp.mean(rows * rows, 1, keepdims=True) + 1e-5)
        out_ref[:, span] = (rows * scale * gain_ref[:, span]).astype(BF16)


def finish_mine_kernel(flags_ref, keep_ref, came_ref, reads_ref, gain_ref, w_ref, out_ref, normed_ref):
    finish_kernel(flags_ref, keep_ref, came_ref, reads_ref, gain_ref, normed_ref)
    out_ref[...] = dot(normed_ref[...], w_ref[...]).astype(BF16)


def hold_kernel(w_ref, held_ref):
    held_ref[...] = w_ref[...]


def output_kernel(theirs_ref, w_ref, mine_ref, out_ref):
    theirs = dot(theirs_ref[...], w_ref[...]).astype(BF16).astype(F32)
    out_ref[...] = (mine_ref[...].astype(F32) + theirs).astype(BF16)


def call(kernel, outs, inputs, scalars=(), scratch=(), flops=10**7, moved=10**5, grant=8):
    specs = [pl.BlockSpec(memory_space=pltpu.SMEM)] * len(scalars)
    specs += [VMEM] * len(inputs)
    return pl.pallas_call(
        kernel,
        out_shape=[jax.ShapeDtypeStruct(shape, dtype) for shape, dtype in outs],
        in_specs=specs,
        out_specs=[VMEM] * len(outs),
        scratch_shapes=list(scratch),
        compiler_params=pltpu.CompilerParams(vmem_limit_bytes=grant * 1024 * 1024),
        cost_estimate=pl.CostEstimate(flops=flops, bytes_accessed=moved, transcendentals=0),
    )(*scalars, *inputs)


def together(*arrays):
    return lax.optimization_barrier(arrays)


def shift(block, axes, pairs):
    return lax.ppermute(block, axes, pairs)


def local(tokens, w_query, w_key, w_value, w_beta, beta_bias, conv_weight, norm_gain, w_out):
    groups = lax.axis_size("head")
    shards = lax.axis_size("seq")
    heads = beta_bias.shape[0]
    columns = w_query.shape[1]
    dim = columns // heads
    width = tokens.shape[1]
    me_head = lax.axis_index("head")
    me_seq = lax.axis_index("seq")
    ahead = [(i, i + 1) for i in range(shards - 1)]

    if groups == 2:
        rows = tokens.shape[0]
        swap = [(0, 1), (1, 0)]
        early = tokens
        late = shift(tokens, "head", swap)
        head, tail = call(
            edge_kernel, [((HALO, width), BF16)] * 2, [tokens], flops=2 * 10**10, moved=10**6
        )
        flat = [(i, i + 1) for i in range(shards * groups - 1)]
        halo = shift(tail, ("seq", "head"), flat)
        behind = shift(tail, "seq", ahead)
        swapped = me_head
    else:
        gathered = lax.all_gather(tokens, "head", axis=0, tiled=True)
        rows = gathered.shape[0] // 2
        early, late = gathered[:rows], gathered[rows:]
        halo = behind = shift(late[rows - HALO :], "seq", ahead)
        head, tail = early[:HALO], early[rows - HALO :]
        swapped = jnp.zeros((), jnp.int32)

    gain = norm_gain.reshape(1, columns)
    pair_shape = (heads, dim, 2 * dim)
    kept = heads // 2 if heads % 2 == 0 else heads
    kept_shape = (kept,) + pair_shape[1:]
    levels = shards.bit_length() - 1
    bits = [((me_seq >> level) & 1).astype(jnp.int32).reshape(1) for level in range(levels)]
    swapped = swapped.astype(jnp.int32).reshape(1)
    weights = [w_query, w_key, w_value, w_beta.T, conv_weight]
    pair0, look0 = call(
        early_kernel,
        [(pair_shape, F32), ((heads, rows, 2 * dim), BF16)],
        [early] + weights,
        scalars=[beta_bias],
        scratch=[pltpu.VMEM((3, rows + HALO, columns), F32)],
        grant=24,
    )
    keep, send, norm, held = call(
        late_kernel,
        [
            (kept_shape, BF16),
            (kept_shape, BF16),
            ((heads, rows), F32),
            ((heads, 2 * rows + 2 * dim + HALO, 2 * dim), BF16),
        ],
        [late] + weights + [head, tail, halo, behind, pair0],
        scalars=[swapped, bits[0], beta_bias],
        scratch=[pltpu.VMEM((3, rows + 3 * HALO, columns), F32)],
        grant=24,
    )
    if groups == 2:
        w_sent, keep = together(w_out, keep)
        w_other = shift(w_sent, "head", swap)
    own = keep
    for level in range(levels):
        partner = [(i, i ^ (1 << level)) for i in range(shards)]
        if level == levels - 1:
            partner = [(i, j) for i, j in partner if j > i]
        came = shift(send, "seq", partner)
        if level == 1:
            late = call(
                look_late_kernel,
                [((heads, rows, 2 * dim), BF16)],
                [norm, held],
                scalars=[swapped],
            )[0]
            came, path, late = together(came, path, late)
        elif level == 2:
            early = call(
                functools.partial(look_early_kernel, conv_weight.shape[1]),
                [((heads, rows, 2 * dim), BF16)],
                [held, look0],
                scalars=[swapped],
            )[0]
            came, path, early = together(came, path, early)
        elif level > 2:
            came, path = together(came, path)
        if level == levels - 1:
            break
        send = call(
            join_kernel,
            [((kept, dim, dim if level == levels - 2 else 2 * dim), BF16)],
            [own, came],
            scalars=[bits[level]],
        )[0]
        if level == 0:
            own, came, send = together(own, came, send)
            path = call(
                open_kernel, [((kept, 2 * dim, 2 * dim), BF16)], [own, came], scalars=[bits[0]]
            )[0]
        else:
            path, came, send = together(path, came, send)
            path = call(
                path_kernel, [((kept, 2 * dim, 2 * dim), BF16)], [path, came], scalars=[bits[level]]
            )[0]
        own = send
    keep, send = call(
        enter_kernel,
        [((kept, dim, dim), BF16)] * 2,
        [came, path],
        scalars=[bits[0], bits[levels - 1]],
    )
    came = shift(send, "seq", [(i, i ^ 1) for i in range(shards)]) if kept < heads else send
    gone = call(
        finish_kernel,
        [((rows, columns), BF16)],
        [keep, came, late, gain],
        scalars=[bits[0]],
    )[0]
    if groups == 2:
        theirs = shift(gone, "head", swap)
        mine = call(
            finish_mine_kernel,
            [((rows, width), BF16)],
            [keep, came, early, gain, w_out],
            scalars=[bits[0]],
            scratch=[pltpu.VMEM((rows, columns), BF16)],
        )[0]
        w_other, gone = together(w_other, gone)
        whole = call(hold_kernel, [(w_out.shape, BF16)], [w_other])[0]
        theirs, whole = together(theirs, whole)
        return call(output_kernel, [((rows, width), BF16)], [theirs, whole, mine])[0]
    normed = call(
        finish_kernel,
        [((rows, columns), BF16)],
        [keep, came, early, gain],
        scalars=[bits[0]],
    )[0]
    product = jnp.dot(
        jnp.concatenate([normed, gone], 0), w_out, preferred_element_type=F32
    ).astype(BF16)
    return lax.psum_scatter(product, "head", scatter_dimension=0, tiled=True)


def solution(mesh):
    in_specs = (
        P(("seq", "head"), None),
        P(None, "head"),
        P(None, "head"),
        P(None, "head"),
        P(None, "head"),
        P("head"),
        P(None, None, "head"),
        P("head"),
        P("head", None),
    )
    out_specs = P(("seq", "head"), None)
    return jax.shard_map(local, mesh=mesh, in_specs=in_specs, out_specs=out_specs, check_vma=False)
```

```python
import functools

import jax
import jax.numpy as jnp
from jax import lax
from jax.experimental import pallas as pl
from jax.experimental.pallas import tpu as pltpu
from jax.sharding import PartitionSpec as P

BASE = 16
HALO = 16
F32 = jnp.float32
BF16 = jnp.bfloat16
VMEM = pl.BlockSpec(memory_space=pltpu.VMEM)
NN = ((1,), (0,))
NT = ((1,), (1,))
TN = ((0,), (0,))


def dot(left, right, dims=NN):
    return lax.dot_general(left, right, (dims, ((), ())), preferred_element_type=F32)


def split(wide):
    top = wide.astype(BF16)
    return top, (wide - top.astype(F32)).astype(BF16)


def dot_wide(left, right, dims=NN):
    left_top, left_rest = split(left)
    right_top, right_rest = split(right)
    return (
        dot(left_top, right_top, dims)
        + dot(left_rest, right_top, dims)
        + dot(left_top, right_rest, dims)
    )


def dot_half(left, right, dims=NN):
    left_top, left_rest = split(left)
    return dot(left_top, right, dims) + dot(left_rest, right, dims)


def substitute(windows):
    lanes = windows[0].shape[0]
    row = lax.broadcasted_iota(jnp.int32, (8, lanes), 0)
    lane = lax.broadcasted_iota(jnp.int32, (8, lanes), 1)
    group = lane // BASE
    bands = BASE // 8
    packed, solved = [], []
    for window in windows:
        rows = []
        for band in range(bands):
            piece = window[band * 8 : band * 8 + 8]
            for index in range(1, lanes // BASE):
                start = index * BASE + band * 8
                piece = jnp.where(group == index, window[start : start + 8], piece)
            rows.append(piece)
        packed.append(rows)
        solved.append(
            [(row + band * 8 == lane - group * BASE).astype(F32) for band in range(bands)]
        )
    for step in range(BASE - 1):
        at = step // 8
        place = group * BASE + step
        for rows, found in zip(packed, solved):
            pivot = found[at][step % 8 : step % 8 + 1]
            for band in range(at, bands):
                if band > at or step % 8 < 7:
                    column = jnp.take_along_axis(rows[band], place, axis=1)
                    found[band] = found[band] - column * pivot
    return [
        jnp.concatenate(
            [jnp.where(group == index, piece, 0.0) for index in range(lanes // BASE) for piece in found],
            0,
        )
        for found in solved
    ]


def invert(lowers):
    size = lowers[0].shape[0]
    lanes = 128
    starts = range(0, size, lanes)
    windows = [low[at : at + lanes, at : at + lanes] for low in lowers for at in starts]
    inverses = substitute(windows)
    row = lax.broadcasted_iota(jnp.int32, (lanes, lanes), 0)
    lane = lax.broadcasted_iota(jnp.int32, (lanes, lanes), 1)
    width = BASE
    while width < lanes:
        mask = (row // (2 * width) == lane // (2 * width)) & (row // width != lane // width)
        picks = range(width, lanes, 2 * width)

        def odd(full):
            return jnp.concatenate([full[at : at + width] for at in picks], 0)

        def spread(picked):
            none = jnp.zeros((width, lanes), F32)
            return jnp.concatenate(
                [
                    each
                    for index in range(len(picks))
                    for each in (none, picked[index * width : (index + 1) * width])
                ],
                0,
            )

        inner = [
            dot_wide(odd(jnp.where(mask, window, 0.0)), inverse)
            for window, inverse in zip(windows, inverses)
        ]
        inverses = [
            inverse - spread(dot_wide(odd(inverse), spread(each)))
            for inverse, each in zip(inverses, inner)
        ]
        width *= 2
    count = len(starts)
    groups = [inverses[at : at + count] for at in range(0, len(inverses), count)]
    while width < size:
        joined = []
        below = [
            [
                dot_wide(
                    low[(at + 1) * width : (at + 2) * width, at * width : (at + 1) * width], parts[at]
                )
                for at in range(0, len(parts), 2)
            ]
            for low, parts in zip(lowers, groups)
        ]
        for inner, parts in zip(below, groups):
            merged = []
            for at in range(0, len(parts), 2):
                first, second = parts[at], parts[at + 1]
                corner = -dot_wide(second, inner[at // 2])
                merged.append(
                    jnp.concatenate(
                        [
                            jnp.concatenate([first, jnp.zeros_like(first)], 1),
                            jnp.concatenate([corner, second], 1),
                        ],
                        0,
                    )
                )
            joined.append(merged)
        groups = joined
        width *= 2
    return [parts[0] for parts in groups]


def activate(x, weights, conv_ref, proj_ref, blocks):
    taps = conv_ref.shape[1]
    active = [[] for _ in blocks]
    for index, w_ref in enumerate(weights):
        proj_ref[index] = dot(x, w_ref[...]).astype(BF16).astype(F32)
        for (start, rows), outs in zip(blocks, active):
            first = start - (taps - 1)
            total = proj_ref[index, first : first + rows] * conv_ref[index, 0:1]
            for tap in range(1, taps):
                total = total + proj_ref[index, first + tap : first + tap + rows] * conv_ref[
                    index, tap : tap + 1
                ]
            outs.append((total / (1.0 + jnp.exp(-total))).astype(BF16))
    return active


def invert_few(count, lowers):
    inverses = []
    for lower in lowers:
        eye = jnp.eye(lower.shape[0], dtype=F32)
        inverse = eye - lower
        for _ in range(count - 2):
            inverse = eye - dot_wide(lower, inverse)
        inverses.append(inverse)
    return inverses


def within(shape, group):
    row = lax.broadcasted_iota(jnp.int32, shape, 0)
    lane = lax.broadcasted_iota(jnp.int32, shape, 1)
    if group is None or group >= shape[0]:
        return row, lane, True
    return row, lane, row // group == lane // group


def solve(keys, values, rates, invert=invert, group=None):
    rows, dim = keys[0].shape
    row, lane, same = within((rows, rows), group)
    norms, norm_rows, lowers = [], [], []
    for key, rate_row in zip(keys, rates):
        rate = jnp.sum(jnp.where(row == lane, rate_row, 0.0), 1, keepdims=True)
        wide_key = key.astype(F32)
        norm = lax.rsqrt(jnp.sum(wide_key * wide_key, 1, keepdims=True) + 1e-6)
        norm_row = jnp.sum(jnp.where(row == lane, norm, 0.0), 0, keepdims=True)
        norms.append(norm)
        norm_rows.append(norm_row)
        gram = dot(key, key, NT)
        lowers.append(jnp.where((row > lane) & same, gram * (rate * norm) * norm_row, 0.0))
    solved = []
    for key, value, inverse, rate_row, norm in zip(keys, values, invert(lowers), rates, norms):
        top, rest = split(inverse * rate_row)
        unit, unit_rest = split(key.astype(F32) * norm)
        both = jnp.concatenate([unit, value], 1)
        each = dot(top, both) + dot(rest, both)
        solved.append(jnp.concatenate([each[:, :dim] + dot(top, unit_rest), each[:, dim:]], 1))
    return solved, norms, norm_rows


def pair_of(key, solved, norm):
    dim = key.shape[1]
    top, rest = split(solved * norm)
    moved = dot(key, top, TN) + dot(key, rest, TN)
    return jnp.concatenate([jnp.eye(dim, dtype=F32) - moved[:, :dim], moved[:, dim:]], 1)


def transitions(keys, values, rates):
    solved, norms, norm_rows = solve(keys, values, rates)
    return [pair_of(*each) for each in zip(keys, solved, norms)], solved, norm_rows


def look(query, key, norm_row, solved, group=None):
    rows, dim = query.shape
    row, lane, same = within((rows, rows), group)
    attend = jnp.where((row >= lane) & same, dot(query, key, NT) * norm_row, 0.0)
    seen = dot_half(attend, solved)
    return jnp.concatenate([query.astype(F32) - seen[:, :dim], seen[:, dim:]], 1)


def spans_of(count, width):
    dim = width // count
    return [slice(head * dim, (head + 1) * dim) for head in range(count)]


def write_rates(x, wb, bias_ref):
    logits = dot(wb, x, NT)
    return [
        2.0 / (1.0 + jnp.exp(-(logits[head : head + 1] + bias_ref[head])))
        for head in range(wb.shape[0])
    ]


def edge_kernel(x_ref, head_ref, tail_ref):
    head_ref[...] = x_ref[: head_ref.shape[0]]
    tail_ref[...] = x_ref[x_ref.shape[0] - tail_ref.shape[0] :]


def half_kernel(bit_ref, w_ref, part_ref):
    part_ref[...] = w_ref[...]


def half_rows(w_out, bit):
    half = (w_out.shape[0] // 2, w_out.shape[1])
    return pl.pallas_call(
        half_kernel,
        grid_spec=pltpu.PrefetchScalarGridSpec(
            num_scalar_prefetch=1,
            grid=(1,),
            in_specs=[pl.BlockSpec(half, lambda at, bit: (bit[0], 0))],
            out_specs=pl.BlockSpec(half, lambda at, bit: (0, 0)),
        ),
        out_shape=jax.ShapeDtypeStruct(half, w_out.dtype),
        cost_estimate=pl.CostEstimate(flops=10**7, bytes_accessed=10**5, transcendentals=0),
    )(bit, w_out)


def early_kernel(
    bias_ref, x_ref, wq_ref, wk_ref, wv_ref, wb_ref, conv_ref, pair_ref, look_ref, proj_ref
):
    rows, width = x_ref.shape
    x = jnp.concatenate([jnp.zeros((HALO, width), BF16), x_ref[...]], 0)
    active = activate(x, (wq_ref, wk_ref, wv_ref), conv_ref, proj_ref, [(HALO, rows)])[0]
    spans = spans_of(pair_ref.shape[0], active[0].shape[1])
    queries, keys, values = ([each[:, span] for span in spans] for each in active)
    lane = lax.broadcasted_iota(jnp.int32, (1, rows), 1)
    rates = [
        jnp.where(lane < conv_ref.shape[1] - 1, 0.0, each)
        for each in write_rates(x_ref[...], wb_ref[...], bias_ref)
    ]
    pairs, solved, norm_rows = transitions(keys, values, rates)
    for head in range(len(spans)):
        pair_ref[head] = pairs[head]
        look_ref[head] = look(
            queries[head], keys[head], norm_rows[head], solved[head].astype(BF16)
        ).astype(BF16)


def late_kernel(
    swapped_ref,
    bit_ref,
    bias_ref,
    x_ref,
    wq_ref,
    wk_ref,
    wv_ref,
    wb_ref,
    conv_ref,
    head_ref,
    tail_ref,
    halo_ref,
    behind_ref,
    early_ref,
    keep_ref,
    send_ref,
    norm_ref,
    held_ref,
    proj_ref,
):
    heads = early_ref.shape[0]
    kept = keep_ref.shape[0]
    rows = x_ref.shape[0]
    swapped = swapped_ref[0] == 1
    halo = jnp.where(swapped, behind_ref[...], tail_ref[...])
    x = jnp.concatenate([halo, x_ref[...], halo_ref[...], head_ref[...]], 0)
    active, few = activate(
        x,
        (wq_ref, wk_ref, wv_ref),
        conv_ref,
        proj_ref,
        [(HALO, rows), (2 * HALO + rows, HALO)],
    )
    spans = spans_of(heads, active[0].shape[1])
    queries, keys, values = ([each[:, span] for span in spans] for each in active)
    rates = write_rates(x_ref[...], wb_ref[...], bias_ref)
    lane = lax.broadcasted_iota(jnp.int32, (1, HALO), 1)
    few_rates = jnp.concatenate(
        [
            jnp.where(lane < conv_ref.shape[1] - 1, each, 0.0)
            for each in write_rates(head_ref[...], wb_ref[...], bias_ref)
        ],
        1,
    )
    stacked = [jnp.concatenate([each[:, span] for span in spans], 0) for each in few]
    few_solved, few_norms, few_norm_row = solve(
        stacked[1:2],
        stacked[2:],
        [few_rates],
        functools.partial(invert_few, conv_ref.shape[1] - 1),
        HALO,
    )
    few_solved, few_norms = few_solved[0], few_norms[0]
    mini = look(stacked[0], stacked[1], few_norm_row[0], few_solved.astype(BF16), HALO)
    few_pairs, early = [], []
    for head in range(heads):
        at = slice(head * HALO, (head + 1) * HALO)
        few_pair = pair_of(stacked[1][at], few_solved[at], few_norms[at])
        few_pairs.append(few_pair.astype(BF16))
        early.append(compose(few_pair, early_ref[head]))
    pairs, solved, norm_rows = transitions(keys, values, rates)
    bit = bit_ref[0]
    wholes = []
    for head, late in enumerate(pairs):
        norm_ref[head : head + 1] = norm_rows[head]
        low = jnp.where(swapped, late, early[head])
        held_ref[head] = jnp.concatenate(
            [
                solved[head].astype(BF16),
                jnp.concatenate([queries[head], keys[head]], 1),
                low.astype(BF16),
                few_pairs[head],
                mini[head * HALO : (head + 1) * HALO].astype(BF16),
            ],
            0,
        )
        wholes.append(compose(low, jnp.where(swapped, early[head], late)).astype(BF16))
    for head in range(kept):
        if kept == heads:
            keep_ref[head] = wholes[head]
            send_ref[head] = wholes[head]
        else:
            one, two = wholes[head], wholes[head + kept]
            keep_ref[head] = jnp.where(bit == 1, two, one)
            send_ref[head] = jnp.where(bit == 1, one, two)


def after(reads, pair):
    dim = pair.shape[0]
    through = dot(reads[:, :dim].astype(BF16), pair)
    return jnp.concatenate([through[:, :dim], through[:, dim:] + reads[:, dim:]], 1)


def look_late_kernel(swapped_ref, norm_ref, held_ref, late_ref):
    heads = held_ref.shape[0]
    rows = norm_ref.shape[1]
    dim = held_ref.shape[2] // 2
    for head in range(heads):
        late = look(
            held_ref[head, rows : 2 * rows, :dim],
            held_ref[head, rows : 2 * rows, dim:],
            norm_ref[head : head + 1],
            held_ref[head, :rows],
        )
        later = after(late, held_ref[head, 2 * rows : 2 * rows + dim])
        late_ref[head] = jnp.where(swapped_ref[0] == 1, late, later).astype(BF16)


def look_early_kernel(taps, swapped_ref, held_ref, early_ref, out_ref):
    heads, rows, wide = early_ref.shape
    dim = wide // 2
    row = lax.broadcasted_iota(jnp.int32, (HALO, wide), 0)
    start = 2 * rows
    for head in range(heads):
        early = after(early_ref[head].astype(F32), held_ref[head, start + dim : start + 2 * dim])
        few = held_ref[head, start + 2 * dim :].astype(F32)
        top = jnp.where(row < taps - 1, few, early[:HALO])
        early = jnp.concatenate([top, early[HALO:]], 0)
        later = after(early, held_ref[head, start : start + dim])
        out_ref[head] = jnp.where(swapped_ref[0] == 1, later, early).astype(BF16)


def compose(low, high):
    dim = low.shape[0]
    joined = dot_wide(high[:, :dim], low)
    return jnp.concatenate([joined[:, :dim], joined[:, dim:] + high[:, dim:]], 1)


def join_kernel(flags_ref, own_ref, other_ref, send_ref):
    later = flags_ref[0] == 1
    for head in range(own_ref.shape[0]):
        own, other = own_ref[head], other_ref[head]
        low = jnp.where(later, other, own)
        high = jnp.where(later, own, other)
        dim = low.shape[0]
        landed = send_ref.shape[2] - dim
        joined = dot(high[:, :dim], low)
        if landed > 0:
            send_ref[head, :, :dim] = joined[:, :dim].astype(BF16)
        send_ref[head, :, landed:] = (joined[:, dim:] + high[:, dim:].astype(F32)).astype(BF16)


def open_kernel(flags_ref, own_ref, other_ref, path_ref):
    dim = own_ref.shape[1]
    row = lax.broadcasted_iota(jnp.int32, (dim, 2 * dim), 0)
    lane = lax.broadcasted_iota(jnp.int32, (dim, 2 * dim), 1)
    for head in range(own_ref.shape[0]):
        path_ref[head, :dim] = (row == lane).astype(BF16)
        low = jnp.where(flags_ref[0] == 1, other_ref[head], own_ref[head])
        path_ref[head, dim:] = low


def path_kernel(flags_ref, path_ref, came_ref, out_ref):
    dim = came_ref.shape[1]
    for head in range(came_ref.shape[0]):
        path = path_ref[head]
        through = dot(path[:, :dim], came_ref[head])
        longer = jnp.concatenate([through[:, :dim], through[:, dim:] + path[:, dim:].astype(F32)], 1)
        out_ref[head] = jnp.where(flags_ref[0] == 1, longer.astype(BF16), path)


def enter_kernel(bit_ref, reached_ref, state_ref, path_ref, keep_ref, send_ref):
    dim = state_ref.shape[1]
    for head in range(keep_ref.shape[0]):
        state = jnp.where(reached_ref[0] == 1, state_ref[head], jnp.zeros_like(state_ref[head]))
        path = path_ref[head]
        both = (dot(path[:, :dim], state) + path[:, dim:].astype(F32)).astype(BF16)
        later = bit_ref[0] == 1
        keep_ref[head] = jnp.where(later, both[dim:], both[:dim])
        send_ref[head] = jnp.where(later, both[:dim], both[dim:])


def finish_kernel(flags_ref, keep_ref, came_ref, reads_ref, gain_ref, out_ref):
    count, dim = keep_ref.shape[:2]
    heads = reads_ref.shape[0]
    for head, span in enumerate(spans_of(heads, heads * dim)):
        state = keep_ref[head % count]
        if count < heads:
            state = jnp.where(flags_ref[0] == head // count, state, came_ref[head % count])
        reach = reads_ref[head, :, :dim]
        rows = reads_ref[head, :, dim:].astype(F32) + dot(reach, state)
        scale = lax.rsqrt(jnp.mean(rows * rows, 1, keepdims=True) + 1e-5)
        out_ref[:, span] = (rows * scale * gain_ref[:, span]).astype(BF16)


def finish_mine_kernel(flags_ref, keep_ref, came_ref, reads_ref, gain_ref, w_ref, out_ref, normed_ref):
    finish_kernel(flags_ref, keep_ref, came_ref, reads_ref, gain_ref, normed_ref)
    out_ref[...] = dot(normed_ref[...], w_ref[...]).astype(BF16)


def hold_kernel(bit_ref, part_ref, rest_ref, whole_ref):
    rows = part_ref.shape[0]
    later = bit_ref[0] == 1
    whole_ref[:rows] = jnp.where(later, rest_ref[...], part_ref[...])
    whole_ref[rows:] = jnp.where(later, part_ref[...], rest_ref[...])


def output_kernel(theirs_ref, w_ref, mine_ref, out_ref):
    theirs = dot(theirs_ref[...], w_ref[...]).astype(BF16).astype(F32)
    out_ref[...] = (mine_ref[...].astype(F32) + theirs).astype(BF16)


def call(kernel, outs, inputs, scalars=(), scratch=(), flops=10**7, moved=10**5, grant=8):
    specs = [pl.BlockSpec(memory_space=pltpu.SMEM)] * len(scalars)
    specs += [VMEM] * len(inputs)
    return pl.pallas_call(
        kernel,
        out_shape=[jax.ShapeDtypeStruct(shape, dtype) for shape, dtype in outs],
        in_specs=specs,
        out_specs=[VMEM] * len(outs),
        scratch_shapes=list(scratch),
        compiler_params=pltpu.CompilerParams(vmem_limit_bytes=grant * 1024 * 1024),
        cost_estimate=pl.CostEstimate(flops=flops, bytes_accessed=moved, transcendentals=0),
    )(*scalars, *inputs)


def together(*arrays):
    return lax.optimization_barrier(arrays)


def shift(block, axes, pairs):
    return lax.ppermute(block, axes, pairs)


def local(tokens, w_query, w_key, w_value, w_beta, beta_bias, conv_weight, norm_gain, w_out):
    groups = lax.axis_size("head")
    shards = lax.axis_size("seq")
    heads = beta_bias.shape[0]
    columns = w_query.shape[1]
    dim = columns // heads
    width = tokens.shape[1]
    me_head = lax.axis_index("head")
    me_seq = lax.axis_index("seq")
    ahead = [(i, i + 1) for i in range(shards - 1)]

    if groups == 2:
        rows = tokens.shape[0]
        swap = [(0, 1), (1, 0)]
        early = tokens
        late = shift(tokens, "head", swap)
        head, tail = call(
            edge_kernel, [((HALO, width), BF16)] * 2, [tokens], flops=2 * 10**10, moved=10**6
        )
        flat = [(i, i + 1) for i in range(shards * groups - 1)]
        halo = shift(tail, ("seq", "head"), flat)
        behind = shift(tail, "seq", ahead)
        swapped = me_head
    else:
        gathered = lax.all_gather(tokens, "head", axis=0, tiled=True)
        rows = gathered.shape[0] // 2
        early, late = gathered[:rows], gathered[rows:]
        halo = behind = shift(late[rows - HALO :], "seq", ahead)
        head, tail = early[:HALO], early[rows - HALO :]
        swapped = jnp.zeros((), jnp.int32)

    gain = norm_gain.reshape(1, columns)
    pair_shape = (heads, dim, 2 * dim)
    kept = heads // 2 if heads % 2 == 0 else heads
    kept_shape = (kept,) + pair_shape[1:]
    levels = shards.bit_length() - 1
    bits = [((me_seq >> level) & 1).astype(jnp.int32).reshape(1) for level in range(levels)]
    swapped = swapped.astype(jnp.int32).reshape(1)
    weights = [w_query, w_key, w_value, w_beta.T, conv_weight]
    pair0, look0 = call(
        early_kernel,
        [(pair_shape, F32), ((heads, rows, 2 * dim), BF16)],
        [early] + weights,
        scalars=[beta_bias],
        scratch=[pltpu.VMEM((3, rows + HALO, columns), F32)],
        grant=24,
    )
    keep, send, norm, held = call(
        late_kernel,
        [
            (kept_shape, BF16),
            (kept_shape, BF16),
            ((heads, rows), F32),
            ((heads, 2 * rows + 2 * dim + HALO, 2 * dim), BF16),
        ],
        [late] + weights + [head, tail, halo, behind, pair0],
        scalars=[swapped, bits[0], beta_bias],
        scratch=[pltpu.VMEM((3, rows + 3 * HALO, columns), F32)],
        grant=24,
    )
    own = keep
    for level in range(levels):
        partner = [(i, i ^ (1 << level)) for i in range(shards)]
        came = shift(send, "seq", partner)
        if level == 1:
            late = call(
                look_late_kernel,
                [((heads, rows, 2 * dim), BF16)],
                [norm, held],
                scalars=[swapped],
            )[0]
            came, path, late = together(came, path, late)
            if groups == 2:
                came, part = together(came, part)
                part = shift(part, "head", swap)
        elif level == 2:
            early = call(
                functools.partial(look_early_kernel, conv_weight.shape[1]),
                [((heads, rows, 2 * dim), BF16)],
                [held, look0],
                scalars=[swapped],
            )[0]
            came, path, early = together(came, path, early)
        elif level > 2:
            came, path = together(came, path)
        if level == levels - 1:
            break
        send = call(
            join_kernel,
            [((kept, dim, dim if level == levels - 2 else 2 * dim), BF16)],
            [own, came],
            scalars=[bits[level]],
        )[0]
        if level == 0:
            own, came, send = together(own, came, send)
            if groups == 2:
                w_sent, send = together(w_out, send)
                part = half_rows(w_sent, bits[0])
            path = call(
                open_kernel, [((kept, 2 * dim, 2 * dim), BF16)], [own, came], scalars=[bits[0]]
            )[0]
        else:
            path, came, send = together(path, came, send)
            path = call(
                path_kernel, [((kept, 2 * dim, 2 * dim), BF16)], [path, came], scalars=[bits[level]]
            )[0]
        own = send
    keep, send = call(
        enter_kernel,
        [((kept, dim, dim), BF16)] * 2,
        [came, path],
        scalars=[bits[0], bits[levels - 1]],
    )
    came = shift(send, "seq", [(i, i ^ 1) for i in range(shards)]) if kept < heads else send
    gone = call(
        finish_kernel,
        [((rows, columns), BF16)],
        [keep, came, late, gain],
        scalars=[bits[0]],
    )[0]
    if groups == 2:
        theirs = shift(gone, "head", swap)
        mine = call(
            finish_mine_kernel,
            [((rows, width), BF16)],
            [keep, came, early, gain, w_out],
            scalars=[bits[0]],
            scratch=[pltpu.VMEM((rows, columns), BF16)],
            grant=62,
            flops=6 * 10**9,
        )[0]
        part, gone = together(part, gone)
        rest = shift(part, "seq", [(i, i ^ 1) for i in range(shards)])
        whole = call(hold_kernel, [(w_out.shape, BF16)], [part, rest], scalars=[bits[0]])[0]
        theirs, whole = together(theirs, whole)
        return call(output_kernel, [((rows, width), BF16)], [theirs, whole, mine])[0]
    normed = call(
        finish_kernel,
        [((rows, columns), BF16)],
        [keep, came, early, gain],
        scalars=[bits[0]],
    )[0]
    product = jnp.dot(
        jnp.concatenate([normed, gone], 0), w_out, preferred_element_type=F32
    ).astype(BF16)
    return lax.psum_scatter(product, "head", scatter_dimension=0, tiled=True)


def solution(mesh):
    in_specs = (
        P(("seq", "head"), None),
        P(None, "head"),
        P(None, "head"),
        P(None, "head"),
        P(None, "head"),
        P("head"),
        P(None, None, "head"),
        P("head"),
        P("head", None),
    )
    out_specs = P(("seq", "head"), None)
    return jax.shard_map(local, mesh=mesh, in_specs=in_specs, out_specs=out_specs, check_vma=False)
```

```python
import functools

import jax
import jax.numpy as jnp
from jax import lax
from jax.experimental import pallas as pl
from jax.experimental.pallas import tpu as pltpu
from jax.sharding import PartitionSpec as P

BASE = 16
HALO = 16
F32 = jnp.float32
BF16 = jnp.bfloat16
VMEM = pl.BlockSpec(memory_space=pltpu.VMEM)
NN = ((1,), (0,))
NT = ((1,), (1,))
TN = ((0,), (0,))


def dot(left, right, dims=NN):
    return lax.dot_general(left, right, (dims, ((), ())), preferred_element_type=F32)


def split(wide):
    top = wide.astype(BF16)
    return top, (wide - top.astype(F32)).astype(BF16)


def dot_wide(left, right, dims=NN):
    left_top, left_rest = split(left)
    right_top, right_rest = split(right)
    return (
        dot(left_top, right_top, dims)
        + dot(left_rest, right_top, dims)
        + dot(left_top, right_rest, dims)
    )


def dot_half(left, right, dims=NN):
    left_top, left_rest = split(left)
    return dot(left_top, right, dims) + dot(left_rest, right, dims)


def substitute(windows):
    lanes = windows[0].shape[0]
    row = lax.broadcasted_iota(jnp.int32, (8, lanes), 0)
    lane = lax.broadcasted_iota(jnp.int32, (8, lanes), 1)
    group = lane // BASE
    bands = BASE // 8
    packed, solved = [], []
    for window in windows:
        rows = []
        for band in range(bands):
            piece = window[band * 8 : band * 8 + 8]
            for index in range(1, lanes // BASE):
                start = index * BASE + band * 8
                piece = jnp.where(group == index, window[start : start + 8], piece)
            rows.append(piece)
        packed.append(rows)
        solved.append(
            [(row + band * 8 == lane - group * BASE).astype(F32) for band in range(bands)]
        )
    for step in range(BASE - 1):
        at = step // 8
        place = group * BASE + step
        for rows, found in zip(packed, solved):
            pivot = found[at][step % 8 : step % 8 + 1]
            for band in range(at, bands):
                if band > at or step % 8 < 7:
                    column = jnp.take_along_axis(rows[band], place, axis=1)
                    found[band] = found[band] - column * pivot
    return [
        jnp.concatenate(
            [jnp.where(group == index, piece, 0.0) for index in range(lanes // BASE) for piece in found],
            0,
        )
        for found in solved
    ]


def invert(lowers):
    size = lowers[0].shape[0]
    lanes = 128
    starts = range(0, size, lanes)
    windows = [low[at : at + lanes, at : at + lanes] for low in lowers for at in starts]
    inverses = substitute(windows)
    row = lax.broadcasted_iota(jnp.int32, (lanes, lanes), 0)
    lane = lax.broadcasted_iota(jnp.int32, (lanes, lanes), 1)
    width = BASE
    while width < lanes:
        mask = (row // (2 * width) == lane // (2 * width)) & (row // width != lane // width)
        picks = range(width, lanes, 2 * width)

        def odd(full):
            return jnp.concatenate([full[at : at + width] for at in picks], 0)

        def spread(picked):
            none = jnp.zeros((width, lanes), F32)
            return jnp.concatenate(
                [
                    each
                    for index in range(len(picks))
                    for each in (none, picked[index * width : (index + 1) * width])
                ],
                0,
            )

        inner = [
            dot_wide(odd(jnp.where(mask, window, 0.0)), inverse)
            for window, inverse in zip(windows, inverses)
        ]
        inverses = [
            inverse - spread(dot_wide(odd(inverse), spread(each)))
            for inverse, each in zip(inverses, inner)
        ]
        width *= 2
    count = len(starts)
    groups = [inverses[at : at + count] for at in range(0, len(inverses), count)]
    while width < size:
        joined = []
        below = [
            [
                dot_wide(
                    low[(at + 1) * width : (at + 2) * width, at * width : (at + 1) * width], parts[at]
                )
                for at in range(0, len(parts), 2)
            ]
            for low, parts in zip(lowers, groups)
        ]
        for inner, parts in zip(below, groups):
            merged = []
            for at in range(0, len(parts), 2):
                first, second = parts[at], parts[at + 1]
                corner = -dot_wide(second, inner[at // 2])
                merged.append(
                    jnp.concatenate(
                        [
                            jnp.concatenate([first, jnp.zeros_like(first)], 1),
                            jnp.concatenate([corner, second], 1),
                        ],
                        0,
                    )
                )
            joined.append(merged)
        groups = joined
        width *= 2
    return [parts[0] for parts in groups]


def activate(x, weights, conv_ref, proj_ref, blocks):
    taps = conv_ref.shape[1]
    active = [[] for _ in blocks]
    for index, w_ref in enumerate(weights):
        proj_ref[index] = dot(x, w_ref[...]).astype(BF16).astype(F32)
        for (start, rows), outs in zip(blocks, active):
            first = start - (taps - 1)
            total = proj_ref[index, first : first + rows] * conv_ref[index, 0:1]
            for tap in range(1, taps):
                total = total + proj_ref[index, first + tap : first + tap + rows] * conv_ref[
                    index, tap : tap + 1
                ]
            outs.append((total / (1.0 + jnp.exp(-total))).astype(BF16))
    return active


def invert_few(count, lowers):
    inverses = []
    for lower in lowers:
        eye = jnp.eye(lower.shape[0], dtype=F32)
        inverse = eye - lower
        for _ in range(count - 2):
            inverse = eye - dot_wide(lower, inverse)
        inverses.append(inverse)
    return inverses


def within(shape, group):
    row = lax.broadcasted_iota(jnp.int32, shape, 0)
    lane = lax.broadcasted_iota(jnp.int32, shape, 1)
    if group is None or group >= shape[0]:
        return row, lane, True
    return row, lane, row // group == lane // group


def solve(keys, values, rates, invert=invert, group=None):
    rows, dim = keys[0].shape
    row, lane, same = within((rows, rows), group)
    norms, norm_rows, lowers = [], [], []
    for key, rate_row in zip(keys, rates):
        rate = jnp.sum(jnp.where(row == lane, rate_row, 0.0), 1, keepdims=True)
        wide_key = key.astype(F32)
        norm = lax.rsqrt(jnp.sum(wide_key * wide_key, 1, keepdims=True) + 1e-6)
        norm_row = jnp.sum(jnp.where(row == lane, norm, 0.0), 0, keepdims=True)
        norms.append(norm)
        norm_rows.append(norm_row)
        gram = dot(key, key, NT)
        lowers.append(jnp.where((row > lane) & same, gram * (rate * norm) * norm_row, 0.0))
    solved = []
    for key, value, inverse, rate_row, norm in zip(keys, values, invert(lowers), rates, norms):
        top, rest = split(inverse * rate_row)
        unit, unit_rest = split(key.astype(F32) * norm)
        both = jnp.concatenate([unit, value], 1)
        each = dot(top, both) + dot(rest, both)
        solved.append(jnp.concatenate([each[:, :dim] + dot(top, unit_rest), each[:, dim:]], 1))
    return solved, norms, norm_rows


def pair_of(key, solved, norm):
    dim = key.shape[1]
    top, rest = split(solved * norm)
    moved = dot(key, top, TN) + dot(key, rest, TN)
    return jnp.concatenate([jnp.eye(dim, dtype=F32) - moved[:, :dim], moved[:, dim:]], 1)


def transitions(keys, values, rates):
    solved, norms, norm_rows = solve(keys, values, rates)
    return [pair_of(*each) for each in zip(keys, solved, norms)], solved, norm_rows


def look(query, key, norm_row, solved, group=None):
    rows, dim = query.shape
    row, lane, same = within((rows, rows), group)
    attend = jnp.where((row >= lane) & same, dot(query, key, NT) * norm_row, 0.0)
    seen = dot_half(attend, solved)
    return jnp.concatenate([query.astype(F32) - seen[:, :dim], seen[:, dim:]], 1)


def spans_of(count, width):
    dim = width // count
    return [slice(head * dim, (head + 1) * dim) for head in range(count)]


def write_rates(x, wb, bias_ref):
    logits = dot(wb, x, NT)
    return [
        2.0 / (1.0 + jnp.exp(-(logits[head : head + 1] + bias_ref[head])))
        for head in range(wb.shape[0])
    ]


def edge_kernel(x_ref, head_ref, tail_ref):
    head_ref[...] = x_ref[: head_ref.shape[0]]
    tail_ref[...] = x_ref[x_ref.shape[0] - tail_ref.shape[0] :]


def half_kernel(bit_ref, w_ref, part_ref):
    part_ref[...] = w_ref[...]


def half_rows(w_out, bit):
    half = (w_out.shape[0] // 2, w_out.shape[1])
    return pl.pallas_call(
        half_kernel,
        grid_spec=pltpu.PrefetchScalarGridSpec(
            num_scalar_prefetch=1,
            grid=(1,),
            in_specs=[pl.BlockSpec(half, lambda at, bit: (bit[0], 0))],
            out_specs=pl.BlockSpec(half, lambda at, bit: (0, 0)),
        ),
        out_shape=jax.ShapeDtypeStruct(half, w_out.dtype),
        cost_estimate=pl.CostEstimate(flops=10**7, bytes_accessed=10**5, transcendentals=0),
    )(bit, w_out)


def early_kernel(
    bias_ref, x_ref, wq_ref, wk_ref, wv_ref, wb_ref, conv_ref, pair_ref, look_ref, proj_ref
):
    rows, width = x_ref.shape
    x = jnp.concatenate([jnp.zeros((HALO, width), BF16), x_ref[...]], 0)
    active = activate(x, (wq_ref, wk_ref, wv_ref), conv_ref, proj_ref, [(HALO, rows)])[0]
    spans = spans_of(pair_ref.shape[0], active[0].shape[1])
    queries, keys, values = ([each[:, span] for span in spans] for each in active)
    lane = lax.broadcasted_iota(jnp.int32, (1, rows), 1)
    rates = [
        jnp.where(lane < conv_ref.shape[1] - 1, 0.0, each)
        for each in write_rates(x_ref[...], wb_ref[...], bias_ref)
    ]
    pairs, solved, norm_rows = transitions(keys, values, rates)
    for head in range(len(spans)):
        pair_ref[head] = pairs[head]
        look_ref[head] = look(
            queries[head], keys[head], norm_rows[head], solved[head].astype(BF16)
        ).astype(BF16)


def late_kernel(
    swapped_ref,
    bit_ref,
    bias_ref,
    x_ref,
    wq_ref,
    wk_ref,
    wv_ref,
    wb_ref,
    conv_ref,
    head_ref,
    tail_ref,
    halo_ref,
    behind_ref,
    early_ref,
    keep_ref,
    send_ref,
    norm_ref,
    held_ref,
    proj_ref,
):
    heads = early_ref.shape[0]
    kept = keep_ref.shape[0]
    rows = x_ref.shape[0]
    swapped = swapped_ref[0] == 1
    halo = jnp.where(swapped, behind_ref[...], tail_ref[...])
    x = jnp.concatenate([halo, x_ref[...], halo_ref[...], head_ref[...]], 0)
    active, few = activate(
        x,
        (wq_ref, wk_ref, wv_ref),
        conv_ref,
        proj_ref,
        [(HALO, rows), (2 * HALO + rows, HALO)],
    )
    spans = spans_of(heads, active[0].shape[1])
    queries, keys, values = ([each[:, span] for span in spans] for each in active)
    rates = write_rates(x_ref[...], wb_ref[...], bias_ref)
    lane = lax.broadcasted_iota(jnp.int32, (1, HALO), 1)
    few_rates = jnp.concatenate(
        [
            jnp.where(lane < conv_ref.shape[1] - 1, each, 0.0)
            for each in write_rates(head_ref[...], wb_ref[...], bias_ref)
        ],
        1,
    )
    stacked = [jnp.concatenate([each[:, span] for span in spans], 0) for each in few]
    few_solved, few_norms, few_norm_row = solve(
        stacked[1:2],
        stacked[2:],
        [few_rates],
        functools.partial(invert_few, conv_ref.shape[1] - 1),
        HALO,
    )
    few_solved, few_norms = few_solved[0], few_norms[0]
    mini = look(stacked[0], stacked[1], few_norm_row[0], few_solved.astype(BF16), HALO)
    few_pairs, early = [], []
    for head in range(heads):
        at = slice(head * HALO, (head + 1) * HALO)
        few_pair = pair_of(stacked[1][at], few_solved[at], few_norms[at])
        few_pairs.append(few_pair.astype(BF16))
        early.append(compose(few_pair, early_ref[head]))
    pairs, solved, norm_rows = transitions(keys, values, rates)
    bit = bit_ref[0]
    wholes = []
    for head, late in enumerate(pairs):
        norm_ref[head : head + 1] = norm_rows[head]
        low = jnp.where(swapped, late, early[head])
        held_ref[head] = jnp.concatenate(
            [
                solved[head].astype(BF16),
                jnp.concatenate([queries[head], keys[head]], 1),
                low.astype(BF16),
                few_pairs[head],
                mini[head * HALO : (head + 1) * HALO].astype(BF16),
            ],
            0,
        )
        wholes.append(compose(low, jnp.where(swapped, early[head], late)).astype(BF16))
    for head in range(kept):
        if kept == heads:
            keep_ref[head] = wholes[head]
            send_ref[head] = wholes[head]
        else:
            one, two = wholes[head], wholes[head + kept]
            keep_ref[head] = jnp.where(bit == 1, two, one)
            send_ref[head] = jnp.where(bit == 1, one, two)


def after(reads, pair):
    dim = pair.shape[0]
    through = dot(reads[:, :dim].astype(BF16), pair)
    return jnp.concatenate([through[:, :dim], through[:, dim:] + reads[:, dim:]], 1)


def look_late_kernel(swapped_ref, norm_ref, held_ref, late_ref):
    heads = held_ref.shape[0]
    rows = norm_ref.shape[1]
    dim = held_ref.shape[2] // 2
    for head in range(heads):
        late = look(
            held_ref[head, rows : 2 * rows, :dim],
            held_ref[head, rows : 2 * rows, dim:],
            norm_ref[head : head + 1],
            held_ref[head, :rows],
        )
        later = after(late, held_ref[head, 2 * rows : 2 * rows + dim])
        late_ref[head] = jnp.where(swapped_ref[0] == 1, late, later).astype(BF16)


def look_early_kernel(taps, swapped_ref, held_ref, early_ref, out_ref):
    heads, rows, wide = early_ref.shape
    dim = wide // 2
    row = lax.broadcasted_iota(jnp.int32, (HALO, wide), 0)
    start = 2 * rows
    for head in range(heads):
        early = after(early_ref[head].astype(F32), held_ref[head, start + dim : start + 2 * dim])
        few = held_ref[head, start + 2 * dim :].astype(F32)
        top = jnp.where(row < taps - 1, few, early[:HALO])
        early = jnp.concatenate([top, early[HALO:]], 0)
        later = after(early, held_ref[head, start : start + dim])
        out_ref[head] = jnp.where(swapped_ref[0] == 1, later, early).astype(BF16)


def compose(low, high):
    dim = low.shape[0]
    joined = dot_wide(high[:, :dim], low)
    return jnp.concatenate([joined[:, :dim], joined[:, dim:] + high[:, dim:]], 1)


def join_kernel(flags_ref, own_ref, other_ref, send_ref):
    later = flags_ref[0] == 1
    for head in range(own_ref.shape[0]):
        own, other = own_ref[head], other_ref[head]
        low = jnp.where(later, other, own)
        high = jnp.where(later, own, other)
        dim = low.shape[0]
        landed = send_ref.shape[2] - dim
        joined = dot(high[:, :dim], low)
        if landed > 0:
            send_ref[head, :, :dim] = joined[:, :dim].astype(BF16)
        send_ref[head, :, landed:] = (joined[:, dim:] + high[:, dim:].astype(F32)).astype(BF16)


def open_kernel(flags_ref, own_ref, other_ref, path_ref):
    dim = own_ref.shape[1]
    row = lax.broadcasted_iota(jnp.int32, (dim, 2 * dim), 0)
    lane = lax.broadcasted_iota(jnp.int32, (dim, 2 * dim), 1)
    for head in range(own_ref.shape[0]):
        path_ref[head, :dim] = (row == lane).astype(BF16)
        low = jnp.where(flags_ref[0] == 1, other_ref[head], own_ref[head])
        path_ref[head, dim:] = low


def path_kernel(flags_ref, path_ref, came_ref, out_ref):
    dim = came_ref.shape[1]
    for head in range(came_ref.shape[0]):
        path = path_ref[head]
        through = dot(path[:, :dim], came_ref[head])
        longer = jnp.concatenate([through[:, :dim], through[:, dim:] + path[:, dim:].astype(F32)], 1)
        out_ref[head] = jnp.where(flags_ref[0] == 1, longer.astype(BF16), path)


def enter_kernel(bit_ref, reached_ref, state_ref, path_ref, keep_ref, send_ref):
    dim = state_ref.shape[1]
    for head in range(keep_ref.shape[0]):
        state = jnp.where(reached_ref[0] == 1, state_ref[head], jnp.zeros_like(state_ref[head]))
        path = path_ref[head]
        both = (dot(path[:, :dim], state) + path[:, dim:].astype(F32)).astype(BF16)
        later = bit_ref[0] == 1
        keep_ref[head] = jnp.where(later, both[dim:], both[:dim])
        send_ref[head] = jnp.where(later, both[:dim], both[dim:])


def normed_rows(state, reads, gain):
    dim = state.shape[0]
    rows = reads[:, dim:].astype(F32) + dot(reads[:, :dim], state)
    scale = lax.rsqrt(jnp.mean(rows * rows, 1, keepdims=True) + 1e-5)
    return (rows * scale * gain).astype(BF16)


def finish_kernel(side, bit_ref, state_ref, reads_ref, gain_ref, out_ref):
    count = state_ref.shape[0]
    own = bit_ref[0] if side == 0 else 1 - bit_ref[0]
    first = own * count if count < reads_ref.shape[0] else 0
    for head, span in enumerate(spans_of(count, out_ref.shape[1])):
        out_ref[:, span] = normed_rows(
            state_ref[head], reads_ref[first + head], gain_ref[first + head]
        )


def finish_mine_kernel(
    bit_ref, keep_ref, came_ref, reads_ref, gain_ref, w_ref, out_ref, normed_ref
):
    size = normed_ref.shape[2]
    total = None
    for side, state_ref in enumerate((keep_ref, came_ref)):
        finish_kernel(side, bit_ref, state_ref, reads_ref, gain_ref, normed_ref.at[side])
        own = bit_ref[0] if side == 0 else 1 - bit_ref[0]
        rows = w_ref[pl.ds(pl.multiple_of(own * size, size), size)]
        each = dot(normed_ref[side], rows)
        total = each if total is None else total + each
    out_ref[...] = total.astype(BF16)


def output_kernel(own_ref, other_ref, w_own_ref, w_other_ref, mine_ref, out_ref):
    total = dot(own_ref[...], w_own_ref[...]) + dot(other_ref[...], w_other_ref[...])
    theirs = total.astype(BF16).astype(F32)
    out_ref[...] = (mine_ref[...].astype(F32) + theirs).astype(BF16)


def call(kernel, outs, inputs, scalars=(), scratch=(), flops=10**7, moved=10**5, grant=8):
    specs = [pl.BlockSpec(memory_space=pltpu.SMEM)] * len(scalars)
    specs += [VMEM] * len(inputs)
    return pl.pallas_call(
        kernel,
        out_shape=[jax.ShapeDtypeStruct(shape, dtype) for shape, dtype in outs],
        in_specs=specs,
        out_specs=[VMEM] * len(outs),
        scratch_shapes=list(scratch),
        compiler_params=pltpu.CompilerParams(vmem_limit_bytes=grant * 1024 * 1024),
        cost_estimate=pl.CostEstimate(flops=flops, bytes_accessed=moved, transcendentals=0),
    )(*scalars, *inputs)


def together(*arrays):
    return lax.optimization_barrier(arrays)


def shift(block, axes, pairs):
    return lax.ppermute(block, axes, pairs)


def local(tokens, w_query, w_key, w_value, w_beta, beta_bias, conv_weight, norm_gain, w_out):
    groups = lax.axis_size("head")
    shards = lax.axis_size("seq")
    heads = beta_bias.shape[0]
    columns = w_query.shape[1]
    dim = columns // heads
    width = tokens.shape[1]
    me_head = lax.axis_index("head")
    me_seq = lax.axis_index("seq")
    ahead = [(i, i + 1) for i in range(shards - 1)]

    kept = heads // 2 if heads % 2 == 0 else heads
    lean = groups == 2 and kept < heads
    if lean:
        rows = tokens.shape[0]
        swap = [(0, 1), (1, 0)]
        early = tokens
        late = shift(tokens, "head", swap)
        head, tail = call(
            edge_kernel, [((HALO, width), BF16)] * 2, [tokens], flops=2 * 10**10, moved=10**6
        )
        flat = [(i, i + 1) for i in range(shards * groups - 1)]
        halo = shift(tail, ("seq", "head"), flat)
        behind = shift(tail, "seq", ahead)
        swapped = me_head
    else:
        gathered = lax.all_gather(tokens, "head", axis=0, tiled=True)
        rows = gathered.shape[0] // 2
        early, late = gathered[:rows], gathered[rows:]
        halo = behind = shift(late[rows - HALO :], "seq", ahead)
        head, tail = early[:HALO], early[rows - HALO :]
        swapped = jnp.zeros((), jnp.int32)

    gain = norm_gain.reshape(heads, 1, dim)
    pair_shape = (heads, dim, 2 * dim)
    kept_shape = (kept,) + pair_shape[1:]
    levels = shards.bit_length() - 1
    bits = [((me_seq >> level) & 1).astype(jnp.int32).reshape(1) for level in range(levels)]
    swapped = swapped.astype(jnp.int32).reshape(1)
    weights = [w_query, w_key, w_value, w_beta.T, conv_weight]
    pair0, look0 = call(
        early_kernel,
        [(pair_shape, F32), ((heads, rows, 2 * dim), BF16)],
        [early] + weights,
        scalars=[beta_bias],
        scratch=[pltpu.VMEM((3, rows + HALO, columns), F32)],
        grant=24,
    )
    keep, send, norm, held = call(
        late_kernel,
        [
            (kept_shape, BF16),
            (kept_shape, BF16),
            ((heads, rows), F32),
            ((heads, 2 * rows + 2 * dim + HALO, 2 * dim), BF16),
        ],
        [late] + weights + [head, tail, halo, behind, pair0],
        scalars=[swapped, bits[0], beta_bias],
        scratch=[pltpu.VMEM((3, rows + 3 * HALO, columns), F32)],
        grant=24,
    )
    own = keep
    for level in range(levels):
        partner = [(i, i ^ (1 << level)) for i in range(shards)]
        came = shift(send, "seq", partner)
        if level == 1:
            late = call(
                look_late_kernel,
                [((heads, rows, 2 * dim), BF16)],
                [norm, held],
                scalars=[swapped],
            )[0]
            came, path, late = together(came, path, late)
            if lean:
                came, part = together(came, part)
                part = shift(part, "head", swap)
        elif level == 2:
            early = call(
                functools.partial(look_early_kernel, conv_weight.shape[1]),
                [((heads, rows, 2 * dim), BF16)],
                [held, look0],
                scalars=[swapped],
            )[0]
            came, path, early = together(came, path, early)
        elif level > 2:
            came, path = together(came, path)
        if level == levels - 1:
            break
        send = call(
            join_kernel,
            [((kept, dim, dim if level == levels - 2 else 2 * dim), BF16)],
            [own, came],
            scalars=[bits[level]],
        )[0]
        if level == 0:
            own, came, send = together(own, came, send)
            if lean:
                w_sent, send = together(w_out, send)
                part = half_rows(w_sent, bits[0])
            path = call(
                open_kernel, [((kept, 2 * dim, 2 * dim), BF16)], [own, came], scalars=[bits[0]]
            )[0]
        else:
            path, came, send = together(path, came, send)
            path = call(
                path_kernel, [((kept, 2 * dim, 2 * dim), BF16)], [path, came], scalars=[bits[level]]
            )[0]
        own = send
    keep, send = call(
        enter_kernel,
        [((kept, dim, dim), BF16)] * 2,
        [came, path],
        scalars=[bits[0], bits[levels - 1]],
    )
    states = [keep]
    if kept < heads:
        states.append(shift(send, "seq", [(i, i ^ 1) for i in range(shards)]))

    def finish(side, reads):
        return call(
            functools.partial(finish_kernel, side),
            [((rows, kept * dim), BF16)],
            [states[side], reads, gain],
            scalars=[bits[0]],
        )[0]

    gone = [finish(side, late) for side in range(len(states))]
    if lean:
        theirs = [shift(each, "head", swap) for each in gone]
        early, theirs[0] = together(early, theirs[0])
        mine = call(
            finish_mine_kernel,
            [((rows, width), BF16)],
            states + [early, gain, w_out],
            scalars=[bits[0]],
            scratch=[pltpu.VMEM((2, rows, kept * dim), BF16)],
            grant=62,
            flops=6 * 10**9,
        )[0]
        part, *_ = together(part, *gone)
        rest = shift(part, "seq", [(i, i ^ 1) for i in range(shards)])
        return call(output_kernel, [((rows, width), BF16)], theirs + [part, rest, mine])[0]
    here = [finish(side, early) for side in range(len(states))]
    normed = [jnp.concatenate(each, 0) for each in zip(here, gone)]
    if len(normed) > 1:
        normed = [jnp.where(bits[0] == side, normed[0], normed[1]) for side in range(2)]
    product = jnp.dot(
        jnp.concatenate(normed, 1), w_out, preferred_element_type=F32
    ).astype(BF16)
    return lax.psum_scatter(product, "head", scatter_dimension=0, tiled=True)


def solution(mesh):
    in_specs = (
        P(("seq", "head"), None),
        P(None, "head"),
        P(None, "head"),
        P(None, "head"),
        P(None, "head"),
        P("head"),
        P(None, None, "head"),
        P("head"),
        P("head", None),
    )
    out_specs = P(("seq", "head"), None)
    return jax.shard_map(local, mesh=mesh, in_specs=in_specs, out_specs=out_specs, check_vma=False)
```

```python
import functools

import jax
import jax.numpy as jnp
from jax import lax
from jax.experimental import pallas as pl
from jax.experimental.pallas import tpu as pltpu
from jax.sharding import PartitionSpec as P

BASE = 16
HALO = 16
F32 = jnp.float32
BF16 = jnp.bfloat16
VMEM = pl.BlockSpec(memory_space=pltpu.VMEM)
NN = ((1,), (0,))
NT = ((1,), (1,))
TN = ((0,), (0,))


def dot(left, right, dims=NN):
    return lax.dot_general(left, right, (dims, ((), ())), preferred_element_type=F32)


def split(wide):
    top = wide.astype(BF16)
    return top, (wide - top.astype(F32)).astype(BF16)


def dot_wide(left, right, dims=NN):
    left_top, left_rest = split(left)
    right_top, right_rest = split(right)
    return (
        dot(left_top, right_top, dims)
        + dot(left_rest, right_top, dims)
        + dot(left_top, right_rest, dims)
    )


def dot_half(left, right, dims=NN):
    left_top, left_rest = split(left)
    return dot(left_top, right, dims) + dot(left_rest, right, dims)


def substitute(windows):
    lanes = windows[0].shape[0]
    row = lax.broadcasted_iota(jnp.int32, (8, lanes), 0)
    lane = lax.broadcasted_iota(jnp.int32, (8, lanes), 1)
    group = lane // BASE
    bands = BASE // 8
    packed, solved = [], []
    for window in windows:
        rows = []
        for band in range(bands):
            piece = window[band * 8 : band * 8 + 8]
            for index in range(1, lanes // BASE):
                start = index * BASE + band * 8
                piece = jnp.where(group == index, window[start : start + 8], piece)
            rows.append(piece)
        packed.append(rows)
        solved.append(
            [(row + band * 8 == lane - group * BASE).astype(F32) for band in range(bands)]
        )
    for step in range(BASE - 1):
        at = step // 8
        place = group * BASE + step
        for rows, found in zip(packed, solved):
            pivot = found[at][step % 8 : step % 8 + 1]
            for band in range(at, bands):
                if band > at or step % 8 < 7:
                    column = jnp.take_along_axis(rows[band], place, axis=1)
                    found[band] = found[band] - column * pivot
    return [
        jnp.concatenate(
            [jnp.where(group == index, piece, 0.0) for index in range(lanes // BASE) for piece in found],
            0,
        )
        for found in solved
    ]


def invert(lowers):
    size = lowers[0].shape[0]
    lanes = 128
    starts = range(0, size, lanes)
    windows = [low[at : at + lanes, at : at + lanes] for low in lowers for at in starts]
    inverses = substitute(windows)
    row = lax.broadcasted_iota(jnp.int32, (lanes, lanes), 0)
    lane = lax.broadcasted_iota(jnp.int32, (lanes, lanes), 1)
    width = BASE
    while width < lanes:
        mask = (row // (2 * width) == lane // (2 * width)) & (row // width != lane // width)
        picks = range(width, lanes, 2 * width)

        def odd(full):
            return jnp.concatenate([full[at : at + width] for at in picks], 0)

        def spread(picked):
            none = jnp.zeros((width, lanes), F32)
            return jnp.concatenate(
                [
                    each
                    for index in range(len(picks))
                    for each in (none, picked[index * width : (index + 1) * width])
                ],
                0,
            )

        inner = [
            dot_wide(odd(jnp.where(mask, window, 0.0)), inverse)
            for window, inverse in zip(windows, inverses)
        ]
        inverses = [
            inverse - spread(dot_wide(odd(inverse), spread(each)))
            for inverse, each in zip(inverses, inner)
        ]
        width *= 2
    count = len(starts)
    groups = [inverses[at : at + count] for at in range(0, len(inverses), count)]
    while width < size:
        joined = []
        below = [
            [
                dot_wide(
                    low[(at + 1) * width : (at + 2) * width, at * width : (at + 1) * width], parts[at]
                )
                for at in range(0, len(parts), 2)
            ]
            for low, parts in zip(lowers, groups)
        ]
        for inner, parts in zip(below, groups):
            merged = []
            for at in range(0, len(parts), 2):
                first, second = parts[at], parts[at + 1]
                corner = -dot_wide(second, inner[at // 2])
                merged.append(
                    jnp.concatenate(
                        [
                            jnp.concatenate([first, jnp.zeros_like(first)], 1),
                            jnp.concatenate([corner, second], 1),
                        ],
                        0,
                    )
                )
            joined.append(merged)
        groups = joined
        width *= 2
    return [parts[0] for parts in groups]


def activate(x, weights, conv_ref, proj_ref, blocks):
    taps = conv_ref.shape[1]
    active = [[] for _ in blocks]
    for index, w_ref in enumerate(weights):
        proj_ref[index] = dot(x, w_ref[...]).astype(BF16).astype(F32)
        for (start, rows), outs in zip(blocks, active):
            first = start - (taps - 1)
            total = proj_ref[index, first : first + rows] * conv_ref[index, 0:1]
            for tap in range(1, taps):
                total = total + proj_ref[index, first + tap : first + tap + rows] * conv_ref[
                    index, tap : tap + 1
                ]
            outs.append((total / (1.0 + jnp.exp(-total))).astype(BF16))
    return active


def invert_few(count, lowers):
    inverses = []
    for lower in lowers:
        eye = jnp.eye(lower.shape[0], dtype=F32)
        inverse = eye - lower
        for _ in range(count - 2):
            inverse = eye - dot_wide(lower, inverse)
        inverses.append(inverse)
    return inverses


def within(shape, group):
    row = lax.broadcasted_iota(jnp.int32, shape, 0)
    lane = lax.broadcasted_iota(jnp.int32, shape, 1)
    if group is None or group >= shape[0]:
        return row, lane, True
    return row, lane, row // group == lane // group


def solve(keys, values, rates, invert=invert, group=None):
    rows, dim = keys[0].shape
    row, lane, same = within((rows, rows), group)
    norms, norm_rows, lowers = [], [], []
    for key, rate_row in zip(keys, rates):
        rate = jnp.sum(jnp.where(row == lane, rate_row, 0.0), 1, keepdims=True)
        wide_key = key.astype(F32)
        norm = lax.rsqrt(jnp.sum(wide_key * wide_key, 1, keepdims=True) + 1e-6)
        norm_row = jnp.sum(jnp.where(row == lane, norm, 0.0), 0, keepdims=True)
        norms.append(norm)
        norm_rows.append(norm_row)
        gram = dot(key, key, NT)
        lowers.append(jnp.where((row > lane) & same, gram * (rate * norm) * norm_row, 0.0))
    solved = []
    for key, value, inverse, rate_row, norm in zip(keys, values, invert(lowers), rates, norms):
        top, rest = split(inverse * rate_row)
        unit, unit_rest = split(key.astype(F32) * norm)
        both = jnp.concatenate([unit, value], 1)
        each = dot(top, both) + dot(rest, both)
        solved.append(jnp.concatenate([each[:, :dim] + dot(top, unit_rest), each[:, dim:]], 1))
    return solved, norms, norm_rows


def pair_of(key, solved, norm):
    dim = key.shape[1]
    top, rest = split(solved * norm)
    moved = dot(key, top, TN) + dot(key, rest, TN)
    return jnp.concatenate([jnp.eye(dim, dtype=F32) - moved[:, :dim], moved[:, dim:]], 1)


def transitions(keys, values, rates):
    solved, norms, norm_rows = solve(keys, values, rates)
    return [pair_of(*each) for each in zip(keys, solved, norms)], solved, norm_rows


def look(query, key, norm_row, solved, group=None):
    rows, dim = query.shape
    row, lane, same = within((rows, rows), group)
    attend = jnp.where((row >= lane) & same, dot(query, key, NT) * norm_row, 0.0)
    seen = dot_half(attend, solved)
    return jnp.concatenate([query.astype(F32) - seen[:, :dim], seen[:, dim:]], 1)


def spans_of(count, width):
    dim = width // count
    return [slice(head * dim, (head + 1) * dim) for head in range(count)]


def write_rates(x, wb, bias_ref):
    logits = dot(wb, x, NT)
    return [
        2.0 / (1.0 + jnp.exp(-(logits[head : head + 1] + bias_ref[head])))
        for head in range(wb.shape[0])
    ]


def edge_kernel(x_ref, head_ref, tail_ref):
    head_ref[...] = x_ref[: head_ref.shape[0]]
    tail_ref[...] = x_ref[x_ref.shape[0] - tail_ref.shape[0] :]


def half_kernel(bit_ref, w_ref, part_ref):
    part_ref[...] = w_ref[...]


def half_rows(w_out, bit):
    half = (w_out.shape[0] // 2, w_out.shape[1])
    return pl.pallas_call(
        half_kernel,
        grid_spec=pltpu.PrefetchScalarGridSpec(
            num_scalar_prefetch=1,
            grid=(1,),
            in_specs=[pl.BlockSpec(half, lambda at, bit: (bit[0], 0))],
            out_specs=pl.BlockSpec(half, lambda at, bit: (0, 0)),
        ),
        out_shape=jax.ShapeDtypeStruct(half, w_out.dtype),
        cost_estimate=pl.CostEstimate(flops=10**7, bytes_accessed=10**5, transcendentals=0),
    )(bit, w_out)


def early_kernel(
    bias_ref, x_ref, wq_ref, wk_ref, wv_ref, wb_ref, conv_ref, pair_ref, look_ref, proj_ref
):
    rows, width = x_ref.shape
    x = jnp.concatenate([jnp.zeros((HALO, width), BF16), x_ref[...]], 0)
    active = activate(x, (wq_ref, wk_ref, wv_ref), conv_ref, proj_ref, [(HALO, rows)])[0]
    spans = spans_of(pair_ref.shape[0], active[0].shape[1])
    queries, keys, values = ([each[:, span] for span in spans] for each in active)
    lane = lax.broadcasted_iota(jnp.int32, (1, rows), 1)
    rates = [
        jnp.where(lane < conv_ref.shape[1] - 1, 0.0, each)
        for each in write_rates(x_ref[...], wb_ref[...], bias_ref)
    ]
    pairs, solved, norm_rows = transitions(keys, values, rates)
    for head in range(len(spans)):
        pair_ref[head] = pairs[head]
        look_ref[head] = look(
            queries[head], keys[head], norm_rows[head], solved[head].astype(BF16)
        ).astype(BF16)


def late_kernel(
    swapped_ref,
    bit_ref,
    bias_ref,
    x_ref,
    wq_ref,
    wk_ref,
    wv_ref,
    wb_ref,
    conv_ref,
    head_ref,
    tail_ref,
    halo_ref,
    behind_ref,
    early_ref,
    keep_ref,
    send_ref,
    norm_ref,
    held_ref,
    proj_ref,
):
    heads = early_ref.shape[0]
    kept = keep_ref.shape[0]
    rows = x_ref.shape[0]
    swapped = swapped_ref[0] == 1
    halo = jnp.where(swapped, behind_ref[...], tail_ref[...])
    x = jnp.concatenate([halo, x_ref[...], halo_ref[...], head_ref[...]], 0)
    active, few = activate(
        x,
        (wq_ref, wk_ref, wv_ref),
        conv_ref,
        proj_ref,
        [(HALO, rows), (2 * HALO + rows, HALO)],
    )
    spans = spans_of(heads, active[0].shape[1])
    queries, keys, values = ([each[:, span] for span in spans] for each in active)
    rates = write_rates(x_ref[...], wb_ref[...], bias_ref)
    lane = lax.broadcasted_iota(jnp.int32, (1, HALO), 1)
    few_rates = jnp.concatenate(
        [
            jnp.where(lane < conv_ref.shape[1] - 1, each, 0.0)
            for each in write_rates(head_ref[...], wb_ref[...], bias_ref)
        ],
        1,
    )
    stacked = [jnp.concatenate([each[:, span] for span in spans], 0) for each in few]
    few_solved, few_norms, few_norm_row = solve(
        stacked[1:2],
        stacked[2:],
        [few_rates],
        functools.partial(invert_few, conv_ref.shape[1] - 1),
        HALO,
    )
    few_solved, few_norms = few_solved[0], few_norms[0]
    mini = look(stacked[0], stacked[1], few_norm_row[0], few_solved.astype(BF16), HALO)
    few_pairs, early = [], []
    for head in range(heads):
        at = slice(head * HALO, (head + 1) * HALO)
        few_pair = pair_of(stacked[1][at], few_solved[at], few_norms[at])
        few_pairs.append(few_pair.astype(BF16))
        early.append(compose(few_pair, early_ref[head]))
    pairs, solved, norm_rows = transitions(keys, values, rates)
    bit = bit_ref[0]
    wholes = []
    for head, late in enumerate(pairs):
        norm_ref[head : head + 1] = norm_rows[head]
        low = jnp.where(swapped, late, early[head])
        held_ref[head] = jnp.concatenate(
            [
                solved[head].astype(BF16),
                jnp.concatenate([queries[head], keys[head]], 1),
                low.astype(BF16),
                few_pairs[head],
                mini[head * HALO : (head + 1) * HALO].astype(BF16),
            ],
            0,
        )
        wholes.append(compose(low, jnp.where(swapped, early[head], late)).astype(BF16))
    for head in range(kept):
        if kept == heads:
            keep_ref[head] = wholes[head]
            send_ref[head] = wholes[head]
        else:
            one, two = wholes[head], wholes[head + kept]
            keep_ref[head] = jnp.where(bit == 1, two, one)
            send_ref[head] = jnp.where(bit == 1, one, two)


def after(reads, pair):
    dim = pair.shape[0]
    through = dot(reads[:, :dim].astype(BF16), pair)
    return jnp.concatenate([through[:, :dim], through[:, dim:] + reads[:, dim:]], 1)


def look_late_kernel(swapped_ref, norm_ref, held_ref, late_ref):
    heads = held_ref.shape[0]
    rows = norm_ref.shape[1]
    dim = held_ref.shape[2] // 2
    for head in range(heads):
        late = look(
            held_ref[head, rows : 2 * rows, :dim],
            held_ref[head, rows : 2 * rows, dim:],
            norm_ref[head : head + 1],
            held_ref[head, :rows],
        )
        later = after(late, held_ref[head, 2 * rows : 2 * rows + dim])
        late_ref[head] = jnp.where(swapped_ref[0] == 1, late, later).astype(BF16)


def look_early_kernel(taps, swapped_ref, held_ref, early_ref, out_ref):
    heads, rows, wide = early_ref.shape
    dim = wide // 2
    row = lax.broadcasted_iota(jnp.int32, (HALO, wide), 0)
    start = 2 * rows
    for head in range(heads):
        early = after(early_ref[head].astype(F32), held_ref[head, start + dim : start + 2 * dim])
        few = held_ref[head, start + 2 * dim :].astype(F32)
        top = jnp.where(row < taps - 1, few, early[:HALO])
        early = jnp.concatenate([top, early[HALO:]], 0)
        later = after(early, held_ref[head, start : start + dim])
        out_ref[head] = jnp.where(swapped_ref[0] == 1, later, early).astype(BF16)


def compose(low, high):
    dim = low.shape[0]
    joined = dot_wide(high[:, :dim], low)
    return jnp.concatenate([joined[:, :dim], joined[:, dim:] + high[:, dim:]], 1)


def join_kernel(flags_ref, own_ref, other_ref, send_ref):
    later = flags_ref[0] == 1
    for head in range(own_ref.shape[0]):
        own, other = own_ref[head], other_ref[head]
        low = jnp.where(later, other, own)
        high = jnp.where(later, own, other)
        dim = low.shape[0]
        landed = send_ref.shape[2] - dim
        joined = dot(high[:, :dim], low)
        if landed > 0:
            send_ref[head, :, :dim] = joined[:, :dim].astype(BF16)
        send_ref[head, :, landed:] = (joined[:, dim:] + high[:, dim:].astype(F32)).astype(BF16)


def open_kernel(flags_ref, own_ref, other_ref, path_ref):
    dim = own_ref.shape[1]
    row = lax.broadcasted_iota(jnp.int32, (dim, 2 * dim), 0)
    lane = lax.broadcasted_iota(jnp.int32, (dim, 2 * dim), 1)
    for head in range(own_ref.shape[0]):
        path_ref[head, :dim] = (row == lane).astype(BF16)
        low = jnp.where(flags_ref[0] == 1, other_ref[head], own_ref[head])
        path_ref[head, dim:] = low


def path_kernel(flags_ref, path_ref, came_ref, out_ref):
    dim = came_ref.shape[1]
    for head in range(came_ref.shape[0]):
        path = path_ref[head]
        through = dot(path[:, :dim], came_ref[head])
        longer = jnp.concatenate([through[:, :dim], through[:, dim:] + path[:, dim:].astype(F32)], 1)
        out_ref[head] = jnp.where(flags_ref[0] == 1, longer.astype(BF16), path)


def enter_kernel(bit_ref, reached_ref, state_ref, path_ref, keep_ref, send_ref):
    dim = state_ref.shape[1]
    for head in range(keep_ref.shape[0]):
        state = jnp.where(reached_ref[0] == 1, state_ref[head], jnp.zeros_like(state_ref[head]))
        path = path_ref[head]
        both = (dot(path[:, :dim], state) + path[:, dim:].astype(F32)).astype(BF16)
        later = bit_ref[0] == 1
        keep_ref[head] = jnp.where(later, both[dim:], both[:dim])
        send_ref[head] = jnp.where(later, both[:dim], both[dim:])


def normed_rows(state, reads, gain):
    dim = state.shape[0]
    rows = reads[:, dim:].astype(F32) + dot(reads[:, :dim], state)
    scale = lax.rsqrt(jnp.mean(rows * rows, 1, keepdims=True) + 1e-5)
    return (rows * scale * gain).astype(BF16)


def finish_kernel(side, bit_ref, state_ref, reads_ref, gain_ref, out_ref):
    count = state_ref.shape[0]
    own = bit_ref[0] if side == 0 else 1 - bit_ref[0]
    first = own * count if count < reads_ref.shape[0] else 0
    for head, span in enumerate(spans_of(count, out_ref.shape[1])):
        out_ref[:, span] = normed_rows(
            state_ref[head], reads_ref[first + head], gain_ref[first + head]
        )


def finish_mine_kernel(
    bit_ref, keep_ref, came_ref, reads_ref, gain_ref, w_ref, out_ref, normed_ref
):
    size = normed_ref.shape[2]
    total = None
    for side, state_ref in enumerate((keep_ref, came_ref)):
        finish_kernel(side, bit_ref, state_ref, reads_ref, gain_ref, normed_ref.at[side])
        own = bit_ref[0] if side == 0 else 1 - bit_ref[0]
        rows = w_ref[pl.ds(pl.multiple_of(own * size, size), size)]
        each = dot(normed_ref[side], rows)
        total = each if total is None else total + each
    out_ref[...] = total.astype(BF16)


def hold_kernel(w_ref, held_ref):
    held_ref[...] = w_ref[...]


def output_kernel(own_ref, other_ref, w_own_ref, w_other_ref, mine_ref, out_ref):
    total = dot(own_ref[...], w_own_ref[...]) + dot(other_ref[...], w_other_ref[...])
    theirs = total.astype(BF16).astype(F32)
    out_ref[...] = (mine_ref[...].astype(F32) + theirs).astype(BF16)


def call(kernel, outs, inputs, scalars=(), scratch=(), flops=10**7, moved=10**5, grant=8):
    specs = [pl.BlockSpec(memory_space=pltpu.SMEM)] * len(scalars)
    specs += [VMEM] * len(inputs)
    return pl.pallas_call(
        kernel,
        out_shape=[jax.ShapeDtypeStruct(shape, dtype) for shape, dtype in outs],
        in_specs=specs,
        out_specs=[VMEM] * len(outs),
        scratch_shapes=list(scratch),
        compiler_params=pltpu.CompilerParams(vmem_limit_bytes=grant * 1024 * 1024),
        cost_estimate=pl.CostEstimate(flops=flops, bytes_accessed=moved, transcendentals=0),
    )(*scalars, *inputs)


def together(*arrays):
    return lax.optimization_barrier(arrays)


def shift(block, axes, pairs):
    return lax.ppermute(block, axes, pairs)


def local(tokens, w_query, w_key, w_value, w_beta, beta_bias, conv_weight, norm_gain, w_out):
    groups = lax.axis_size("head")
    shards = lax.axis_size("seq")
    heads = beta_bias.shape[0]
    columns = w_query.shape[1]
    dim = columns // heads
    width = tokens.shape[1]
    me_head = lax.axis_index("head")
    me_seq = lax.axis_index("seq")
    ahead = [(i, i + 1) for i in range(shards - 1)]

    kept = heads // 2 if heads % 2 == 0 else heads
    lean = groups == 2 and kept < heads
    if lean:
        rows = tokens.shape[0]
        swap = [(0, 1), (1, 0)]
        early = tokens
        late = shift(tokens, "head", swap)
        head, tail = call(
            edge_kernel, [((HALO, width), BF16)] * 2, [tokens], flops=2 * 10**10, moved=10**6
        )
        flat = [(i, i + 1) for i in range(shards * groups - 1)]
        halo = shift(tail, ("seq", "head"), flat)
        behind = shift(tail, "seq", ahead)
        swapped = me_head
    else:
        gathered = lax.all_gather(tokens, "head", axis=0, tiled=True)
        rows = gathered.shape[0] // 2
        early, late = gathered[:rows], gathered[rows:]
        halo = behind = shift(late[rows - HALO :], "seq", ahead)
        head, tail = early[:HALO], early[rows - HALO :]
        swapped = jnp.zeros((), jnp.int32)

    gain = norm_gain.reshape(heads, 1, dim)
    pair_shape = (heads, dim, 2 * dim)
    kept_shape = (kept,) + pair_shape[1:]
    levels = shards.bit_length() - 1
    bits = [((me_seq >> level) & 1).astype(jnp.int32).reshape(1) for level in range(levels)]
    swapped = swapped.astype(jnp.int32).reshape(1)
    weights = [w_query, w_key, w_value, w_beta.T, conv_weight]
    pair0, look0 = call(
        early_kernel,
        [(pair_shape, F32), ((heads, rows, 2 * dim), BF16)],
        [early] + weights,
        scalars=[beta_bias],
        scratch=[pltpu.VMEM((3, rows + HALO, columns), F32)],
        grant=24,
    )
    keep, send, norm, held = call(
        late_kernel,
        [
            (kept_shape, BF16),
            (kept_shape, BF16),
            ((heads, rows), F32),
            ((heads, 2 * rows + 2 * dim + HALO, 2 * dim), BF16),
        ],
        [late] + weights + [head, tail, halo, behind, pair0],
        scalars=[swapped, bits[0], beta_bias],
        scratch=[pltpu.VMEM((3, rows + 3 * HALO, columns), F32)],
        grant=24,
    )
    own = keep
    for level in range(levels):
        partner = [(i, i ^ (1 << level)) for i in range(shards)]
        came = shift(send, "seq", partner)
        if level == 1:
            late = call(
                look_late_kernel,
                [((heads, rows, 2 * dim), BF16)],
                [norm, held],
                scalars=[swapped],
            )[0]
            came, path, late = together(came, path, late)
            if lean:
                came, part = together(came, part)
                part = shift(part, "head", swap)
        elif level == 2:
            early = call(
                functools.partial(look_early_kernel, conv_weight.shape[1]),
                [((heads, rows, 2 * dim), BF16)],
                [held, look0],
                scalars=[swapped],
            )[0]
            came, path, early = together(came, path, early)
        elif level > 2:
            came, path = together(came, path)
        if level == levels - 1:
            break
        send = call(
            join_kernel,
            [((kept, dim, dim if level == levels - 2 else 2 * dim), BF16)],
            [own, came],
            scalars=[bits[level]],
        )[0]
        if level == 0:
            own, came, send = together(own, came, send)
            if lean:
                w_sent, send = together(w_out, send)
                part = half_rows(w_sent, bits[0])
            path = call(
                open_kernel, [((kept, 2 * dim, 2 * dim), BF16)], [own, came], scalars=[bits[0]]
            )[0]
        else:
            path, came, send = together(path, came, send)
            path = call(
                path_kernel, [((kept, 2 * dim, 2 * dim), BF16)], [path, came], scalars=[bits[level]]
            )[0]
        own = send
    keep, send = call(
        enter_kernel,
        [((kept, dim, dim), BF16)] * 2,
        [came, path],
        scalars=[bits[0], bits[levels - 1]],
    )
    states = [keep]
    if kept < heads:
        states.append(shift(send, "seq", [(i, i ^ 1) for i in range(shards)]))

    def finish(side, reads):
        return call(
            functools.partial(finish_kernel, side),
            [((rows, kept * dim), BF16)],
            [states[side], reads, gain],
            scalars=[bits[0]],
        )[0]

    gone = [finish(side, late) for side in range(len(states))]
    if lean:
        theirs = [shift(each, "head", swap) for each in gone]
        w_mine, *_ = together(w_out, *gone)
        w_mine = call(hold_kernel, [(w_out.shape, BF16)], [w_mine], grant=62)[0]
        early, theirs[0], w_mine = together(early, theirs[0], w_mine)
        mine = call(
            finish_mine_kernel,
            [((rows, width), BF16)],
            states + [early, gain, w_mine],
            scalars=[bits[0]],
            scratch=[pltpu.VMEM((2, rows, kept * dim), BF16)],
            flops=6 * 10**9,
        )[0]
        part, *_ = together(part, *gone)
        rest = shift(part, "seq", [(i, i ^ 1) for i in range(shards)])
        return call(output_kernel, [((rows, width), BF16)], theirs + [part, rest, mine])[0]
    here = [finish(side, early) for side in range(len(states))]
    normed = [jnp.concatenate(each, 0) for each in zip(here, gone)]
    if len(normed) > 1:
        normed = [jnp.where(bits[0] == side, normed[0], normed[1]) for side in range(2)]
    product = jnp.dot(
        jnp.concatenate(normed, 1), w_out, preferred_element_type=F32
    ).astype(BF16)
    return lax.psum_scatter(product, "head", scatter_dimension=0, tiled=True)


def solution(mesh):
    in_specs = (
        P(("seq", "head"), None),
        P(None, "head"),
        P(None, "head"),
        P(None, "head"),
        P(None, "head"),
        P("head"),
        P(None, None, "head"),
        P("head"),
        P("head", None),
    )
    out_specs = P(("seq", "head"), None)
    return jax.shard_map(local, mesh=mesh, in_specs=in_specs, out_specs=out_specs, check_vma=False)
```
